128 devices in a mesh: tm: 4 (over x), sys: 32 (over z, y, core).
Axes of the slice: x: 4, y: 4, z: 4, core: 2. Of those that a mesh axis runs over, the one named last changes fastest.
Arguments:
- readings: float32 [8192, 16384], P('sys', 'tm'), may hold values from -20 to 60, as said below
- missing: int32 [8192, 16384], P('sys', 'tm'), may hold values 0 or 1
- left_init: float32 [8192, 64], P('sys'), may hold values from -6 to 6
- right_init: float32 [16384, 64], P('tm'), may hold values from -0.75 to 0.75
Outputs:
- left_factor: float32 [8192, 64], P('sys')
- right_factor: float32 [16384, 64], P('tm')
- sparse: float32 [8192, 16384], P('sys', 'tm')
- dual_var: float32 [8192, 16384], P('sys', 'tm')
The draws below stay inside these ranges and needn't reach their ends.
Inputs may be any that keep to these rules, and one draw needn't show every extreme that they name: Power readings, rough from entry to entry.
All inputs are finite; a program needn't handle non-finite values. No bound on the sum of `missing` on one device may be relied on, other than what follows from the above.
Results may differ from the reference program's by a relative error of at most 0.0003.
Values sent between devices are 32-bit elements; how exact they have to be, the bound alone decides.
A program may use at most 64 MiB of HBM per device.

```python
import math
import jax
import jax.numpy as jnp
from jax import lax

R = 64
ITERS = 2
SYSTEMS = 8192
TIMES = 16384


def draw_readings(key, part):
    keys = jax.random.split(key, 5)
    row_pos = jnp.arange(SYSTEMS, dtype=jnp.int32).astype(jnp.float32)[:, None]
    col_pos = (jnp.arange(TIMES, dtype=jnp.int32) % 96).astype(jnp.float32)[None, :]
    capacity = jnp.exp(jax.random.uniform(keys[0], (SYSTEMS, 1), jnp.float32, 0.0, math.log(10.0)))
    noise = 0.2 * jax.random.normal(keys[1], (SYSTEMS, TIMES), jnp.float32)
    capacity = capacity * (1.0 + 2.0 * row_pos / SYSTEMS)
    daylight = 0.55 - 0.45 * jnp.cos(2.0 * math.pi * col_pos / 96.0)
    cloud = jax.random.uniform(keys[2], (SYSTEMS, TIMES), jnp.float32, 0.3, 1.0)
    spike_on = jax.random.uniform(keys[3], (SYSTEMS, TIMES), jnp.float32) < 0.02
    spikes = jnp.where(spike_on, 3.0 * jax.random.normal(keys[4], (SYSTEMS, TIMES), jnp.float32), 0.0)
    values = capacity * daylight * cloud + noise + spikes
    return jnp.clip(values, -20.0, 60.0).astype(jnp.float32)


def plant(array, stream_key, smallest, high):
    index_at = [jax.random.randint(jax.random.fold_in(stream_key, axis), (), 0, length) for axis, length in enumerate(array.shape)]
    main_axis = array.shape.index(max(array.shape))
    beside = index_at[:main_axis] + [(index_at[main_axis] + 1) % array.shape[main_axis]] + index_at[main_axis + 1:]
    return array.at[tuple(index_at)].set(smallest).at[tuple(beside)].set(high)


def level_of(rng, dims, cuts, smallest, largest):
    def one(dim, parts):
        heights = jax.random.uniform(jax.random.fold_in(jax.random.fold_in(rng, 6), dim), (parts,), jnp.float32, smallest / len(cuts), largest / len(cuts))
        return jnp.repeat(jnp.exp(heights), dims[dim] // parts).reshape((-1,) + (1,) * (len(dims) - dim - 1))

    level = one(*cuts[0])
    for cut in cuts[1:]:
        level = level * one(*cut)
    return level


def bell_draw(own_key, shape, spread, most, shards=(), kind=jnp.bfloat16):
    factor_of = level_of(own_key, shape, shards, -0.22, 0.18) if shards else 1.0
    entries = jax.random.normal(own_key, shape, jnp.float32) * spread * factor_of
    return jnp.minimum(jnp.maximum(entries, -most), most).astype(kind)


def setup_inputs(seed: int = 0) -> dict:
    splits = jax.random.split(jax.random.key(seed), 5)
    readings = draw_readings(jax.random.fold_in(splits[4], 71), 0)
    missing = plant((jax.random.randint(splits[1], (SYSTEMS, TIMES), 0, 10) < 1).astype(jnp.int32), jax.random.fold_in(splits[1], 1), 0, 1)
    left_init = bell_draw(splits[2], (SYSTEMS, R), 1.0, 6.0, ((0, 32),), jnp.float32)
    right_init = bell_draw(splits[3], (TIMES, R), 0.125, 0.75, ((0, 4),), jnp.float32)
    return {"readings": readings, "missing": missing, "left_init": left_init, "right_init": right_init}


def matmul_high(first_op, second_op):
    return jnp.dot(first_op.astype(jnp.float32), second_op.astype(jnp.float32), precision=lax.Precision.HIGHEST, preferred_element_type=jnp.float32)

def ridge_solve(gram, right_side):
    factor = jnp.linalg.cholesky(gram)
    return jax.scipy.linalg.cho_solve((factor, True), right_side.T).T

def reference(readings, missing, left_init, right_init):
    observed_mask = missing == 0
    total_count = jnp.sum(observed_mask.astype(jnp.float32))
    abs_total = jnp.sum(jnp.where(observed_mask, jnp.abs(readings), 0.0))
    penalty = total_count / (4.0 * abs_total + 1e-06)
    sparsity_weight = 1.0 / math.sqrt(max(SYSTEMS, TIMES))
    identity = jnp.eye(R, dtype=jnp.float32)
    left_factor = left_init
    right_factor = right_init
    sparse = jnp.zeros_like(readings)
    dual_var = jnp.zeros_like(readings)
    for sweep in range(ITERS):
        low_rank = matmul_high(left_factor, right_factor.T)
        target = jnp.where(observed_mask, readings - sparse + dual_var / penalty, low_rank)
        gram_v = matmul_high(right_factor.T, right_factor) + identity
        left_factor = ridge_solve(gram_v, matmul_high(target, right_factor))
        gram_u = matmul_high(left_factor.T, left_factor) + identity
        right_factor = ridge_solve(gram_u, matmul_high(target.T, left_factor))
        low_rank = matmul_high(left_factor, right_factor.T)
        shifted = readings - low_rank + dual_var / penalty
        shrunk = jnp.sign(shifted) * jnp.maximum(jnp.abs(shifted) - sparsity_weight / penalty, 0.0)
        sparse = jnp.where(observed_mask, shrunk, 0.0)
        dual_var = jnp.where(observed_mask, dual_var + penalty * (readings - low_rank - sparse), 0.0)
        penalty = 1.5 * penalty
    return (left_factor, right_factor, sparse, dual_var)
```

```python
import functools
import math

import jax
import jax.numpy as jnp
from jax import lax
from jax.experimental import pallas as pl
from jax.experimental.pallas import tpu as pltpu
from jax.sharding import PartitionSpec as P

F32 = jnp.float32
BF16 = jnp.bfloat16
HIGH = lax.Precision.HIGHEST
MESH = pl.DeviceIdType.MESH
VMEM = pltpu.VMEM
RANK = 64
LANES = 128
ABSENT = 1e30
BLOCK = 512
MIB = 1 << 20


def split(value, parts):
    pieces = []
    for part in range(parts):
        piece = value.astype(BF16)
        pieces.append(piece)
        if part + 1 < parts:
            value = value - piece.astype(F32)
    return pieces


def dot(first_op, second_op):
    return jnp.dot(first_op, second_op, preferred_element_type=F32)


def dot_high(first_op, second_op):
    return jnp.dot(first_op, second_op, precision=HIGH, preferred_element_type=F32)


def dot_rows(first_op, second_op):
    return lax.dot_general(
        first_op, second_op, (((0,), (0,)), ((), ())), precision=HIGH, preferred_element_type=F32
    )


def dot_lanes(first_op, second_op, precision=None):
    return lax.dot_general(
        first_op,
        second_op,
        (((1,), (1,)), ((), ())),
        precision=precision,
        preferred_element_type=F32,
    )


def fold(wide):
    half = wide.shape[0] // 2
    return jnp.concatenate([wide[:half], wide[half:]], axis=1)


def unfold(packed):
    return jnp.concatenate([packed[:, :RANK], packed[:, RANK:]], axis=0)


def identity():
    row = lax.broadcasted_iota(jnp.int32, (RANK, RANK), 0)
    col = lax.broadcasted_iota(jnp.int32, (RANK, RANK), 1)
    return jnp.where(row == col, 1.0, 0.0).astype(F32)


def spd_inverse(gram):
    row = lax.broadcasted_iota(jnp.int32, (RANK, LANES), 0)

    def eliminate(_, both):
        cols = [jnp.broadcast_to(both[:, j : j + 1], (RANK, LANES)) for j in range(8)]
        for j in range(8):
            over = 1.0 / cols[j][j : j + 1, :]
            here = row == j
            pivot_row = both[j : j + 1, :] * over
            both = jnp.where(here, pivot_row, both - cols[j] * pivot_row)
            for later in range(j + 1, 8):
                entry = cols[later][j : j + 1, :] * over
                cols[later] = jnp.where(here, entry, cols[later] - cols[j] * entry)
        both = jnp.concatenate([both[8:], both[:8]], axis=0)
        return pltpu.roll(both, LANES - 8, 1)

    both = jnp.concatenate([gram, identity()], axis=1)
    return lax.fori_loop(0, RANK // 8, eliminate, both)[:, :RANK]


def threshold_of(sums, weight):
    count = jnp.sum(sums[0:1, :], axis=1, keepdims=True)
    total = jnp.sum(sums[1:2, :], axis=1, keepdims=True)
    penalty = count / (4.0 * total + 1e-06)
    return penalty, weight / penalty


def first_pass(readings, missing, left, right, seen, high, low_part, message, acc, gram, sums):
    step = pl.program_id(0)

    @pl.when(step == 0)
    def _():
        acc[...] = jnp.zeros_like(acc)
        gram[...] = jnp.zeros_like(gram)
        sums[...] = jnp.zeros_like(sums)

    left_a, left_b = split(left[...], 2)
    rows = right[...]
    right_a, right_b, right_c = split(rows, 3)
    low = dot_lanes(
        jnp.concatenate([left_a, left_a, left_b, left_b], axis=1),
        jnp.concatenate([right_a, right_b, right_a, right_b], axis=1),
    )
    observed = missing[...] == 0
    value = readings[...]
    seen[...] = jnp.where(observed, value, ABSENT)
    target = jnp.where(observed, value, low)
    target_a, target_b = split(target, 2)
    high[...] = target_a
    low_part[...] = target_b
    acc[...] += dot(target_a, jnp.concatenate([right_a, right_b, right_c], axis=1))
    acc[:, :LANES] += dot(target_b, jnp.concatenate([right_a, right_b], axis=1))
    gram[...] += dot_rows(rows, rows)
    count = jnp.sum(jnp.where(observed, 1.0, 0.0), axis=0, keepdims=True)
    total = jnp.sum(jnp.where(observed, jnp.abs(value), 0.0), axis=0, keepdims=True)
    for piece in range(BLOCK // LANES):
        at = slice(piece * LANES, (piece + 1) * LANES)
        sums[0:1, :] += count[:, at]
        sums[1:2, :] += total[:, at]

    @pl.when(step == pl.num_programs(0) - 1)
    def _():
        left_sums = acc[:, :RANK] + acc[:, RANK : 2 * RANK] + acc[:, 2 * RANK :]
        message[0:128, :] = fold(left_sums)
        message[128:160, :] = fold(gram[...])
        message[160:168, :] = sums[...]


def middle_pass(weight, seen, left, right, sums, clipped, scaled, message, acc, gram):
    step = pl.program_id(0)

    @pl.when(step == 0)
    def _():
        acc[...] = jnp.zeros_like(acc)
        gram[...] = jnp.zeros_like(gram)

    _, bound = threshold_of(sums[...], weight)
    left_a, left_b = split(left[...], 2)
    cols = jnp.concatenate([right[i] for i in range(BLOCK // LANES)], axis=1)
    right_a, right_b = split(cols, 2)
    low = dot(
        jnp.concatenate([left_a, left_a, left_b, left_b], axis=1),
        jnp.concatenate([right_a, right_b, right_a, right_b], axis=0),
    )
    value = seen[...]
    inside = jnp.maximum(jnp.minimum(value - low, bound), -bound)
    inside = jnp.where(value < 0.5 * ABSENT, inside, 0.0)
    clipped[...] = inside
    ratio = (inside * (1.0 / bound)).astype(BF16)
    scaled[...] = ratio
    acc[...] += dot_lanes(ratio, jnp.concatenate([right_a, right_b], axis=0))
    gram[...] += dot_lanes(cols, cols, HIGH)

    @pl.when(step == pl.num_programs(0) - 1)
    def _():
        left_sums = (acc[:, :RANK] + acc[:, RANK:]) * ((5.0 / 3.0) * bound)
        message[0:128, :] = fold(left_sums)
        message[128:160, :] = fold(gram[...])
        message[160:168, :] = jnp.zeros((8, LANES), F32)


def last_pass(weight, seen, clipped, left, right, sums, sparse, dual, right_out, left_out):
    penalty, bound = threshold_of(sums[...], weight)
    left_a, left_b = split(left[...], 2)
    cols = jnp.concatenate([right[i] for i in range(BLOCK // LANES)], axis=1)
    right_a, right_b = split(cols, 2)
    low = dot(
        jnp.concatenate([left_a, left_a, left_b, left_b], axis=1),
        jnp.concatenate([right_a, right_b, right_a, right_b], axis=0),
    )
    value = seen[...]
    present = value < 0.5 * ABSENT
    shifted = value - low + clipped[...] * (1.0 / 1.5)
    bound = bound / 1.5
    inside = jnp.maximum(jnp.minimum(shifted, bound), -bound)
    sparse[...] = jnp.where(present, shifted - inside, 0.0)
    dual[...] = jnp.where(present, inside * (1.5 * penalty), 0.0)
    right_out[...] = cols.T
    left_out[...] = left[...]


def exchange(first, weight, *refs):
    if first:
        message, high, low_part, left_out, right_out, sums_out = refs[:6]
        scratch = refs[6:]
    else:
        message, scaled, left_in, right_in, sums_in, left_out, right_out = refs[:7]
        scratch = refs[7:]
    (total, x_recv, gram_send, gram_core, gram_y, gram_z, partial, from_core, recv_a, recv_b, part_a,
     part_b, recv_a2, recv_b2, x_sems, g_sems, c_sems, s_sems, a_sems, f_sems) = scratch

    tm = lax.axis_index("tm")
    me = lax.axis_index("sys")
    core = me % 2
    y = (me // 2) % 4
    z = me // 8

    def at_sys(z_pos, y_pos, core_pos):
        return {"sys": (z_pos * 4 + y_pos) * 2 + core_pos}

    twin = at_sys(z, y, 1 - core)
    y_peer = [None] + [(y + k) % 4 for k in (1, 2, 3)]
    z_peer = [None] + [(z + k) % 4 for k in (1, 2, 3)]
    y_dev = [None] + [at_sys(z, y_peer[k], core) for k in (1, 2, 3)]
    z_dev = [None] + [at_sys(z_peer[k], y, core) for k in (1, 2, 3)]
    x_dev = [{"tm": tm + 1 - 2 * (tm % 2)}, {"tm": 3 - tm}]

    barrier = pltpu.get_barrier_semaphore()
    everyone = x_dev + [twin] + y_dev[1:] + z_dev[1:]
    for device in everyone:
        pl.semaphore_signal(barrier, inc=1, device_id=device, device_id_type=MESH)
    pl.semaphore_wait(barrier, len(everyone))

    def send(src, dst, sems, index, device):
        copy = pltpu.make_async_remote_copy(
            src_ref=src, dst_ref=dst, send_sem=sems.at[0, index], recv_sem=sems.at[1, index],
            device_id=device, device_id_type=MESH,
        )
        copy.start()
        return copy

    halves = (slice(0, 80), slice(80, 168))
    source = message
    for step in range(2):
        copies = [
            send(source.at[halves[h]], x_recv.at[step, halves[h]], x_sems, 2 * step + h, x_dev[(step + h) % 2])
            for h in range(2)
        ]
        for copy in copies:
            copy.wait()
        for h in range(2):
            total[step, halves[h]] = source[halves[h]] + x_recv[step, halves[h]]
        source = total.at[step]
    summed = total[1]
    left_sums = unfold(summed[0:128])
    inverse_v = spd_inverse(unfold(summed[128:160]) + identity())
    if first:
        left = dot_high(left_sums, inverse_v)
        beside = jnp.zeros((RANK, RANK), F32)
    else:
        before = left_in[...]
        left = before + dot_high(left_sums - before, inverse_v)
        beside = dot_rows(left, before)
    left_out[...] = left

    gram_send[0, 0:64, :] = jnp.concatenate([dot_rows(left, left), beside], axis=1)
    gram_send[0, 64:72, :] = summed[160:168]
    gram_copy = send(gram_send.at[0], gram_core, g_sems, 0, twin)

    left_a, left_b, left_c = split(left.T, 3)
    stacked_two = jnp.concatenate([left_a, left_b], axis=0)
    stacked_three = jnp.concatenate([left_a, left_b, left_c], axis=0)

    def products(half, group):
        at = pl.ds(pl.multiple_of(half * 2048 + group * BLOCK, BLOCK), BLOCK)
        if first:
            wide = dot(stacked_three, high[:, at])
            small = dot(stacked_two, low_part[:, at])
            value = wide[0:64] + (wide[64:128] + (wide[128:192] + (small[0:64] + small[64:128])))
        else:
            wide = dot(stacked_two, scaled[:, at])
            value = wide[0:64] + wide[64:128]
        for i in range(4):
            partial[half, group, i] = value[:, i * LANES : (i + 1) * LANES]

    core_copies = []
    for group in range(4):
        products(1 - core, group)
        core_copies.append(
            send(partial.at[1 - core, group], from_core.at[group], c_sems, group, twin)
        )
    for group in range(4):
        products(core, group)

    gram_copy.wait()
    gram_send[1] = gram_send[0] + gram_core[...]
    copies = [send(gram_send.at[1], gram_y.at[k - 1], g_sems, k, y_dev[k]) for k in (1, 2, 3)]
    for group in range(4):
        core_copies[group].wait()
        partial[core, group] += from_core[group]
    for copy in copies:
        copy.wait()
    gram_send[2] = gram_send[1] + gram_y[0] + (gram_y[1] + gram_y[2])
    copies = [send(gram_send.at[2], gram_z.at[k - 1], g_sems, 3 + k, z_dev[k]) for k in (1, 2, 3)]
    first_a = [
        send(partial.at[core, y_peer[k], :, 0:32], recv_a.at[k - 1], s_sems, k - 1, y_dev[k]) for k in (1, 2, 3)
    ]
    first_b = [
        send(partial.at[core, :, z_peer[k], 32:64], recv_b.at[k - 1], s_sems, 2 + k, z_dev[k]) for k in (1, 2, 3)
    ]
    for copy in copies:
        copy.wait()
    grams = gram_send[2] + gram_z[0] + (gram_z[1] + gram_z[2])
    inverse_u = spd_inverse(grams[0:64, 0:64] + identity())

    for copy in first_a:
        copy.wait()
    part_a[...] = partial[core, y, :, 0:32] + recv_a[0] + (recv_a[1] + recv_a[2])
    second = [send(part_a.at[z_peer[k]], recv_a2.at[k - 1], s_sems, 5 + k, z_dev[k]) for k in (1, 2, 3)]
    for copy in first_b:
        copy.wait()
    part_b[...] = partial[core, :, z, 32:64] + recv_b[0] + (recv_b[1] + recv_b[2])
    second += [send(part_b.at[y_peer[k]], recv_b2.at[k - 1], s_sems, 8 + k, y_dev[k]) for k in (1, 2, 3)]
    for copy in second:
        copy.wait()
    sums_a = part_a[z] + recv_a2[0] + (recv_a2[1] + recv_a2[2])
    sums_b = part_b[y] + recv_b2[0] + (recv_b2[1] + recv_b2[2])
    right_sums = jnp.concatenate([sums_a, sums_b], axis=0)
    if first:
        sums_out[...] = grams[64:72]
    else:
        _, bound = threshold_of(sums_in[...], weight)
        right_sums = right_sums * ((5.0 / 3.0) * bound) + dot_high(grams[0:64, 64:128], right_in[core, y, z])
    right_out[core, y, z] = dot_high(inverse_u, right_sums)

    mine = right_out.at[core, y, z]
    to_twin = [send(mine, mine, f_sems, 0, twin)]
    gather_a = [send(mine.at[0:32], mine.at[0:32], a_sems, k - 1, z_dev[k]) for k in (1, 2, 3)]
    gather_b = [send(mine.at[32:64], mine.at[32:64], a_sems, 2 + k, y_dev[k]) for k in (1, 2, 3)]
    for copy in gather_a:
        copy.wait()
    row_a = right_out.at[core, y, :, 0:32]
    last_a = [send(row_a, row_a, a_sems, 5 + k, y_dev[k]) for k in (1, 2, 3)]
    for copy in gather_b:
        copy.wait()
    row_b = right_out.at[core, :, z, 32:64]
    last_b = [send(row_b, row_b, a_sems, 8 + k, z_dev[k]) for k in (1, 2, 3)]
    for k in (1, 2, 3):
        here = right_out.at[core, y, (z + 4 - k) % 4, 0:32]
        to_twin.append(send(here, here, f_sems, k, twin))
        here = right_out.at[core, (y + 4 - k) % 4, z, 32:64]
        to_twin.append(send(here, here, f_sems, 3 + k, twin))
    for k in (1, 2, 3):
        last_a[k - 1].wait()
        here = right_out.at[core, (y + 4 - k) % 4, :, 0:32]
        to_twin.append(send(here, here, f_sems, 6 + k, twin))
        last_b[k - 1].wait()
        here = right_out.at[core, :, (z + 4 - k) % 4, 32:64]
        to_twin.append(send(here, here, f_sems, 9 + k, twin))
    for copy in to_twin:
        copy.wait()


def whole():
    return pl.BlockSpec(memory_space=VMEM)


def params(limit, **more):
    return pltpu.CompilerParams(vmem_limit_bytes=limit * MIB, **more)


def exchange_call(first, weight, *operands):
    dma = pltpu.SemaphoreType.DMA
    shapes = [
        jax.ShapeDtypeStruct((256, RANK), F32),
        jax.ShapeDtypeStruct((2, 4, 4, RANK, LANES), F32),
    ]
    if first:
        shapes.append(jax.ShapeDtypeStruct((8, LANES), F32))
    return pl.pallas_call(
        functools.partial(exchange, first, weight),
        out_shape=shapes,
        in_specs=[whole()] * len(operands),
        out_specs=[whole()] * len(shapes),
        scratch_shapes=[
            VMEM((2, 168, LANES), F32),
            VMEM((2, 168, LANES), F32),
            VMEM((3, 72, LANES), F32),
            VMEM((72, LANES), F32),
            VMEM((3, 72, LANES), F32),
            VMEM((3, 72, LANES), F32),
            VMEM((2, 4, 4, RANK, LANES), F32),
            VMEM((4, 4, RANK, LANES), F32),
            VMEM((3, 4, 32, LANES), F32),
            VMEM((3, 4, 32, LANES), F32),
            VMEM((4, 32, LANES), F32),
            VMEM((4, 32, LANES), F32),
            VMEM((3, 32, LANES), F32),
            VMEM((3, 32, LANES), F32),
            dma((2, 4)),
            dma((2, 7)),
            dma((2, 4)),
            dma((2, 12)),
            dma((2, 12)),
            dma((2, 13)),
        ],
        compiler_params=params(24, collective_id=0 if first else 1, has_side_effects=True),
        cost_estimate=pl.CostEstimate(flops=10**9, bytes_accessed=10**7, transcendentals=0),
    )(*operands)


def on_device(weight, readings, missing, left_init, right_init):
    rows, times = readings.shape
    steps = times // BLOCK
    tile = pl.BlockSpec((rows, BLOCK), lambda i: (0, i))
    fixed = lambda *shape: pl.BlockSpec(shape, lambda i: (0,) * len(shape))
    chunks = pl.BlockSpec((BLOCK // LANES, RANK, LANES), lambda i: (i, 0, 0))
    time_rows = pl.BlockSpec((BLOCK, RANK), lambda i: (i, 0))
    full = lambda kind: jax.ShapeDtypeStruct((rows, times), kind)
    message_shape = jax.ShapeDtypeStruct((168, LANES), F32)

    seen, high, low_part, message = pl.pallas_call(
        first_pass,
        grid=(steps,),
        out_shape=[full(F32), full(BF16), full(BF16), message_shape],
        in_specs=[tile, tile, fixed(rows, RANK), time_rows],
        out_specs=[tile, tile, tile, fixed(168, LANES)],
        scratch_shapes=[VMEM((rows, 3 * RANK), F32), VMEM((RANK, RANK), F32), VMEM((8, LANES), F32)],
        compiler_params=params(24),
    )(readings, missing, left_init, right_init)
    left, right, sums = exchange_call(True, weight, message, high, low_part)
    flat = lambda value: value.reshape(32, RANK, LANES)
    clipped, scaled, message = pl.pallas_call(
        functools.partial(middle_pass, weight),
        grid=(steps,),
        out_shape=[full(F32), full(BF16), message_shape],
        in_specs=[tile, fixed(rows, RANK), chunks, fixed(8, LANES)],
        out_specs=[tile, tile, fixed(168, LANES)],
        scratch_shapes=[VMEM((rows, 2 * RANK), F32), VMEM((RANK, RANK), F32)],
        compiler_params=params(24),
    )(seen, left, flat(right), sums)
    left, right = exchange_call(False, weight, message, scaled, left, right, sums)
    sparse, dual, right_factor, left_factor = pl.pallas_call(
        functools.partial(last_pass, weight),
        grid=(steps,),
        out_shape=[
            full(F32), full(F32), jax.ShapeDtypeStruct((times, RANK), F32),
            jax.ShapeDtypeStruct((rows, RANK), F32),
        ],
        in_specs=[tile, tile, fixed(rows, RANK), chunks, fixed(8, LANES)],
        out_specs=[tile, tile, time_rows, fixed(rows, RANK)],
        compiler_params=params(24),
    )(seen, clipped, left, flat(right), sums)
    return left_factor, right_factor, sparse, dual


def solution(mesh):
    weight = 1.0 / math.sqrt(max(8192, 16384))
    in_specs = (P("sys", "tm"), P("sys", "tm"), P("sys", None), P("tm", None))
    out_specs = (P("sys", None), P("tm", None), P("sys", "tm"), P("sys", "tm"))
    return jax.shard_map(
        functools.partial(on_device, weight), mesh=mesh, in_specs=in_specs, out_specs=out_specs, check_vma=False
    )
```

```python
import functools
import math

import jax
import jax.numpy as jnp
from jax import lax
from jax.experimental import pallas as pl
from jax.experimental.pallas import tpu as pltpu
from jax.sharding import PartitionSpec as P

F32 = jnp.float32
BF16 = jnp.bfloat16
HIGH = lax.Precision.HIGHEST
MESH = pl.DeviceIdType.MESH
VMEM = pltpu.VMEM
RANK = 64
LANES = 128
ABSENT = 1e30
BLOCK = 512
MIB = 1 << 20


def split(value, parts):
    pieces = []
    for part in range(parts):
        piece = value.astype(BF16)
        pieces.append(piece)
        if part + 1 < parts:
            value = value - piece.astype(F32)
    return pieces


def dot(first_op, second_op):
    return jnp.dot(first_op, second_op, preferred_element_type=F32)


def dot_high(first_op, second_op):
    return jnp.dot(first_op, second_op, precision=HIGH, preferred_element_type=F32)


def dot_rows(first_op, second_op):
    return lax.dot_general(
        first_op, second_op, (((0,), (0,)), ((), ())), precision=HIGH, preferred_element_type=F32
    )


def dot_lanes(first_op, second_op, precision=None):
    return lax.dot_general(
        first_op,
        second_op,
        (((1,), (1,)), ((), ())),
        precision=precision,
        preferred_element_type=F32,
    )


def fold(wide):
    half = wide.shape[0] // 2
    return jnp.concatenate([wide[:half], wide[half:]], axis=1)


def unfold(packed):
    return jnp.concatenate([packed[:, :RANK], packed[:, RANK:]], axis=0)


def identity():
    row = lax.broadcasted_iota(jnp.int32, (RANK, RANK), 0)
    col = lax.broadcasted_iota(jnp.int32, (RANK, RANK), 1)
    return jnp.where(row == col, 1.0, 0.0).astype(F32)


def spd_inverse(gram):
    row = lax.broadcasted_iota(jnp.int32, (RANK, LANES), 0)

    def eliminate(_, both):
        cols = [jnp.broadcast_to(both[:, j : j + 1], (RANK, LANES)) for j in range(8)]
        for j in range(8):
            over = 1.0 / cols[j][j : j + 1, :]
            here = row == j
            pivot_row = both[j : j + 1, :] * over
            both = jnp.where(here, pivot_row, both - cols[j] * pivot_row)
            for later in range(j + 1, 8):
                entry = cols[later][j : j + 1, :] * over
                cols[later] = jnp.where(here, entry, cols[later] - cols[j] * entry)
        both = jnp.concatenate([both[8:], both[:8]], axis=0)
        return pltpu.roll(both, LANES - 8, 1)

    both = jnp.concatenate([gram, identity()], axis=1)
    return lax.fori_loop(0, RANK // 8, eliminate, both)[:, :RANK]


def threshold_of(sums, weight):
    count = jnp.sum(sums[0:1, :], axis=1, keepdims=True)
    total = jnp.sum(sums[1:2, :], axis=1, keepdims=True)
    penalty = count / (4.0 * total + 1e-06)
    return penalty, weight / penalty


def left_stack(left):
    first, second = split(left, 2)
    return jnp.concatenate([first, first, second, second], axis=1)


def low_rank(stacked_left, first, second):
    return dot(stacked_left, jnp.concatenate([first, second, first, second], axis=0))


def block_at(half, group):
    return pl.ds(pl.multiple_of(half * 2048 + group * BLOCK, BLOCK), BLOCK)


def join_chunks(chunks, half, group):
    return jnp.concatenate([chunks[half, group, i] for i in range(4)], axis=1)


def factorize(weight, *refs):
    readings, missing, left_in, right_in, seen, clipped, left_out, right_out, sums_out = refs[:9]
    (miss, high, low_part, scaled, right_start, left_start, acc, gram_sum, sums, x_gram, x_gram_in, x_sums,
     x_sums_in, gram_send, gram_core, gram_y, gram_z, partial, from_core, arrived, right_mid, sems, load_sems) = refs[9:]
    used = [0]
    tm = lax.axis_index("tm")
    me = lax.axis_index("sys")
    core = me % 2
    y = (me // 2) % 4
    z = me // 8
    ring = (2, 1, 3)

    def at_sys(z_pos, y_pos, core_pos):
        return {"sys": (z_pos * 4 + y_pos) * 2 + core_pos}

    twin = at_sys(z, y, 1 - core)
    x_dev = {k: {"tm": (tm + k) % 4} for k in ring}
    y_dev = {k: at_sys(z, (y + k) % 4, core) for k in ring}
    z_dev = {k: at_sys((z + k) % 4, y, core) for k in ring}
    plane = {
        (ky, kz): at_sys((z + kz) % 4, (y + ky) % 4, core)
        for ky in range(4) for kz in range(4) if ky or kz
    }

    def send(src, dst, device):
        index = used[0]
        used[0] += 1
        copy = pltpu.make_async_remote_copy(
            src_ref=src, dst_ref=dst, send_sem=sems.at[0, index], recv_sem=sems.at[1, index],
            device_id=device, device_id_type=MESH,
        )
        copy.start()
        return copy

    def load(src, dst, index):
        copy = pltpu.make_async_copy(src, dst, load_sems.at[index])
        copy.start()
        return copy

    small_loads = [load(right_in, right_start, 0), load(left_in, left_start, 1)]
    blocks = [slice(j * BLOCK, (j + 1) * BLOCK) for j in range(8)]
    loads = [
        (load(readings.at[:, at], seen.at[:, at], 2 + 2 * j), load(missing.at[:, at], miss.at[:, at], 3 + 2 * j))
        for j, at in enumerate(blocks)
    ]
    barrier = pltpu.get_barrier_semaphore()
    everyone = list(x_dev.values()) + [twin] + list(plane.values())
    for device in everyone:
        pl.semaphore_signal(barrier, inc=1, device_id=device, device_id_type=MESH)
    for copy in small_loads:
        copy.wait()

    def send_gram(turn, gram):
        x_gram[turn] = fold(gram)
        return [send(x_gram.at[turn], x_gram_in.at[turn, k - 1], x_dev[k]) for k in ring]

    def send_sums(turn):
        return [send(x_sums.at[turn], x_sums_in.at[turn, k - 1], x_dev[k]) for k in ring]

    def finish_gram(turn, copies):
        for copy in copies:
            copy.wait()
        total = (x_gram[turn] + x_gram_in[turn, 0]) + (x_gram_in[turn, 1] + x_gram_in[turn, 2])
        return spd_inverse(unfold(total) + identity())

    def finish_sums(turn, copies):
        for copy in copies:
            copy.wait()
        return (x_sums[turn] + x_sums_in[turn, 0]) + (x_sums_in[turn, 1] + x_sums_in[turn, 2])

    gram = jnp.zeros((RANK, RANK), F32)
    for at in blocks:
        gram += dot_lanes(right_start[:, at], right_start[:, at], HIGH)
    pl.semaphore_wait(barrier, len(everyone))
    gram_copies = send_gram(0, gram)
    stacked_left = left_stack(left_start[...].T)
    acc[...] = jnp.zeros_like(acc)
    sums[...] = jnp.zeros_like(sums)
    for at, copies in zip(blocks, loads):
        right_a, right_b, right_c = split(right_start[:, at], 3)
        low = low_rank(stacked_left, right_a, right_b)
        for copy in copies:
            copy.wait()
        observed = miss[:, at] == 0
        value = seen[:, at]
        seen[:, at] = jnp.where(observed, value, ABSENT)
        target_a, target_b = split(jnp.where(observed, value, low), 2)
        high[:, at] = target_a
        low_part[:, at] = target_b
        acc[...] += dot_lanes(target_a, jnp.concatenate([right_a, right_b, right_c], axis=0))
        acc[:, :LANES] += dot_lanes(target_b, jnp.concatenate([right_a, right_b], axis=0))
        count = jnp.sum(jnp.where(observed, 1.0, 0.0), axis=0, keepdims=True)
        total = jnp.sum(jnp.where(observed, jnp.abs(value), 0.0), axis=0, keepdims=True)
        for piece in range(BLOCK // LANES):
            lanes = slice(piece * LANES, (piece + 1) * LANES)
            sums[0:1, :] += count[:, lanes]
            sums[1:2, :] += total[:, lanes]
    x_sums[0, 0:128, :] = fold(acc[:, :RANK] + acc[:, RANK : 2 * RANK] + acc[:, 2 * RANK :])
    x_sums[0, 128:136, :] = sums[...]
    sum_copies = send_sums(0)
    inverse = finish_gram(0, gram_copies)
    summed = finish_sums(0, sum_copies)
    left = dot_high(unfold(summed[0:128]), inverse)
    left_out[0] = left.T

    def update_right(turn, left, extra, products, finish, target):
        gram_send[turn, 0, 0:32, :] = fold(dot_rows(left, left))
        gram_send[turn, 0, 32:40, :] = extra
        gram_copy = send(gram_send.at[turn, 0], gram_core.at[turn], twin)
        order = (2, 1, 3, 0)
        core_copies = {}
        for ky in order:
            group = (y + ky) % 4
            products(1 - core, group)
            core_copies[ky] = send(partial.at[turn, 1 - core, group], from_core.at[turn, ky], twin)
        gram_copy.wait()
        gram_send[turn, 1] = gram_send[turn, 0] + gram_core[turn]
        y_copies = [send(gram_send.at[turn, 1], gram_y.at[turn, k - 1], y_dev[k]) for k in ring]
        scattered = []
        for ky in order:
            group = (y + ky) % 4
            products(core, group)
            core_copies[ky].wait()
            partial[turn, core, group] += from_core[turn, ky]
            for kz in order:
                if ky or kz:
                    scattered.append(
                        send(partial.at[turn, core, group, (z + kz) % 4], arrived.at[turn, 4 * ky + kz - 1],
                             plane[ky, kz])
                    )
        for copy in y_copies:
            copy.wait()
        gram_send[turn, 2] = (gram_send[turn, 1] + gram_y[turn, 0]) + (gram_y[turn, 1] + gram_y[turn, 2])
        z_copies = [send(gram_send.at[turn, 2], gram_z.at[turn, k - 1], z_dev[k]) for k in ring]
        for copy in z_copies:
            copy.wait()
        grams = (gram_send[turn, 2] + gram_z[turn, 0]) + (gram_z[turn, 1] + gram_z[turn, 2])
        inverse = spd_inverse(unfold(grams[0:32]) + identity())
        finish(grams[32:40])
        for copy in scattered:
            copy.wait()
        total = partial[turn, core, y, z]
        for k in range(0, 15, 3):
            total += (arrived[turn, k] + arrived[turn, k + 1]) + arrived[turn, k + 2]
        target[core, y, z] = dot_high(inverse, total)
        mine = target.at[core, y, z]
        gather = {}
        for ky in order:
            for kz in order:
                if ky or kz:
                    gather[ky, kz] = send(mine, mine, plane[ky, kz])
        near_first = (0, 1, 3, 2)
        to_twin = {}
        for ky in near_first:
            for kz in near_first:
                if ky or kz:
                    gather[ky, kz].wait()
            group = (y + 4 - ky) % 4
            here = target.at[core, group]
            to_twin[ky] = send(here, here, twin)
            yield core, group
        for ky in near_first:
            to_twin[ky].wait()
        for ky in near_first:
            yield 1 - core, (y + 4 - ky) % 4

    def finish_first(total):
        sums_out[...] = total

    stack_a, stack_b, stack_c = split(left.T, 3)
    stacked_two = jnp.concatenate([stack_a, stack_b], axis=0)
    stacked_three = jnp.concatenate([stack_a, stack_b, stack_c], axis=0)

    def products_first(half, group):
        at = block_at(half, group)
        wide = dot(stacked_three, high[:, at])
        small = dot(stacked_two, low_part[:, at])
        value = wide[0:64] + (wide[64:128] + (wide[128:192] + (small[0:64] + small[64:128])))
        for i in range(4):
            partial[0, half, group, i] = value[:, i * LANES : (i + 1) * LANES]

    stacked_left = left_stack(left)
    acc[...] = jnp.zeros_like(acc)
    gram_sum[...] = jnp.zeros_like(gram_sum)
    seen_blocks = 0
    waiting = []
    gram_copies = None

    def middle(half, group):
        _, bound = threshold_of(sums_out[...], weight)
        at = block_at(half, group)
        right_a, right_b = split(join_chunks(right_mid, half, group), 2)
        low = low_rank(stacked_left, right_a, right_b)
        value = seen[:, at]
        inside = jnp.maximum(jnp.minimum(value - low, bound), -bound)
        inside = jnp.where(value < 0.5 * ABSENT, inside, 0.0)
        clipped[:, at] = inside
        ratio = (inside * (1.0 / bound)).astype(BF16)
        scaled[:, at] = ratio
        acc[:, :LANES] += dot_lanes(ratio, jnp.concatenate([right_a, right_b], axis=0))

    for half, group in update_right(0, left, summed[128:136], products_first, finish_first, right_mid):
        cols = join_chunks(right_mid, half, group)
        gram_sum[...] += dot_lanes(cols, cols, HIGH)
        seen_blocks += 1
        if seen_blocks <= 4:
            middle(half, group)
        else:
            waiting.append((half, group))
    gram_copies = send_gram(1, gram_sum[...])
    for half, group in waiting:
        middle(half, group)
    _, bound = threshold_of(sums_out[...], weight)
    scale = (5.0 / 3.0) * bound
    x_sums[1, 0:128, :] = fold((acc[:, :RANK] + acc[:, RANK : 2 * RANK]) * scale)
    x_sums[1, 128:136, :] = jnp.zeros((8, LANES), F32)
    sum_copies = send_sums(1)
    inverse = finish_gram(1, gram_copies)
    summed = finish_sums(1, sum_copies)
    before = left
    left = before + dot_high(unfold(summed[0:128]) - before, inverse)
    left_out[1] = left.T
    mix_a, mix_b, mix_c = split(dot_rows(left, before), 3)
    mixed = jnp.concatenate([mix_a, mix_a, mix_b, mix_c], axis=1)
    last_a, last_b = split(left.T, 2)
    stacked_last = jnp.concatenate([last_a, last_b], axis=0)

    def products_last(half, group):
        at = block_at(half, group)
        wide = dot(stacked_last, scaled[:, at])
        right_a, right_b = split(join_chunks(right_mid, half, group), 2)
        value = dot(mixed, jnp.concatenate([right_a, right_b, right_a, right_a], axis=0))
        value += (wide[0:64] + wide[64:128]) * scale
        for i in range(4):
            partial[1, half, group, i] = value[:, i * LANES : (i + 1) * LANES]

    for _ in update_right(1, left, jnp.zeros((8, LANES), F32), products_last, lambda total: None, right_out):
        pass


def last_pass(weight, seen, clipped, left, right, sums, sparse, dual, right_t, left_t):
    penalty, bound = threshold_of(sums[...], weight)
    cols = jnp.concatenate([right[i] for i in range(BLOCK // LANES)], axis=1)
    right_a, right_b = split(cols, 2)
    low = low_rank(left_stack(left[1].T), right_a, right_b)
    value = seen[...]
    present = value < 0.5 * ABSENT
    shifted = value - low + clipped[...] * (1.0 / 1.5)
    bound = bound / 1.5
    inside = jnp.maximum(jnp.minimum(shifted, bound), -bound)
    sparse[...] = jnp.where(present, shifted - inside, 0.0)
    dual[...] = jnp.where(present, inside * (1.5 * penalty), 0.0)
    right_t[...] = cols
    left_t[...] = left[1]


def params(limit, **more):
    return pltpu.CompilerParams(vmem_limit_bytes=limit * MIB, **more)


def on_device(weight, readings, missing, left_init, right_init):
    rows, times = readings.shape
    steps = times // BLOCK
    shape = jax.ShapeDtypeStruct
    full = shape((rows, times), F32)
    dma = pltpu.SemaphoreType.DMA
    in_vmem = pl.BlockSpec(memory_space=VMEM)
    in_hbm = pl.BlockSpec(memory_space=pltpu.HBM)
    chunked = (2, 4, 4, RANK, LANES)
    seen, clipped, left, right, sums = pl.pallas_call(
        functools.partial(factorize, weight),
        out_shape=[full, full, shape((2, RANK, rows), F32), shape(chunked, F32), shape((8, LANES), F32)],
        in_specs=[in_hbm] * 4,
        out_specs=[in_vmem] * 5,
        scratch_shapes=[
            VMEM((rows, times), jnp.int32),
            VMEM((rows, times), BF16),
            VMEM((rows, times), BF16),
            VMEM((rows, times), BF16),
            VMEM((RANK, times), F32),
            VMEM((RANK, rows), F32),
            VMEM((rows, 3 * RANK), F32),
            VMEM((RANK, RANK), F32),
            VMEM((8, LANES), F32),
            VMEM((2, 32, LANES), F32),
            VMEM((2, 3, 32, LANES), F32),
            VMEM((2, 136, LANES), F32),
            VMEM((2, 3, 136, LANES), F32),
            VMEM((2, 3, 40, LANES), F32),
            VMEM((2, 40, LANES), F32),
            VMEM((2, 3, 40, LANES), F32),
            VMEM((2, 3, 40, LANES), F32),
            VMEM((2,) + chunked, F32),
            VMEM((2, 4, 4, RANK, LANES), F32),
            VMEM((2, 15, RANK, LANES), F32),
            VMEM(chunked, F32),
            dma((2, 102)),
            dma((18,)),
        ],
        compiler_params=params(40, collective_id=0, has_side_effects=True),
    )(readings, missing, left_init.T, right_init.T)
    tile = pl.BlockSpec((rows, BLOCK), lambda i: (0, i))
    fixed = lambda *dims: pl.BlockSpec(dims, lambda i: (0,) * len(dims))
    sparse, dual, right_t, left_t = pl.pallas_call(
        functools.partial(last_pass, weight),
        grid=(steps,),
        out_shape=[full, full, shape((RANK, times), F32), shape((RANK, rows), F32)],
        in_specs=[
            tile, tile, fixed(2, RANK, rows),
            pl.BlockSpec((BLOCK // LANES, RANK, LANES), lambda i: (i, 0, 0)), fixed(8, LANES),
        ],
        out_specs=[tile, tile, pl.BlockSpec((RANK, BLOCK), lambda i: (0, i)), fixed(RANK, rows)],
        compiler_params=params(24),
    )(seen, clipped, left, right.reshape(32, RANK, LANES), sums)
    return left_t.T, right_t.T, sparse, dual


def solution(mesh):
    weight = 1.0 / math.sqrt(max(8192, 16384))
    in_specs = (P("sys", "tm"), P("sys", "tm"), P("sys", None), P("tm", None))
    out_specs = (P("sys", None), P("tm", None), P("sys", "tm"), P("sys", "tm"))
    return jax.shard_map(
        functools.partial(on_device, weight), mesh=mesh, in_specs=in_specs, out_specs=out_specs, check_vma=False
    )
```

```python
import functools
import math

import jax
import jax.numpy as jnp
from jax import lax
from jax.experimental import pallas as pl
from jax.experimental.pallas import tpu as pltpu
from jax.sharding import PartitionSpec as P

F32 = jnp.float32
BF16 = jnp.bfloat16
HIGH = lax.Precision.HIGHEST
MESH = pl.DeviceIdType.MESH
VMEM = pltpu.VMEM
RANK = 64
LANES = 128
ABSENT = 1e30
BLOCK = 512
MIB = 1 << 20


def split(value, parts):
    pieces = []
    for part in range(parts):
        piece = value.astype(BF16)
        pieces.append(piece)
        if part + 1 < parts:
            value = value - piece.astype(F32)
    return pieces


def dot(first_op, second_op):
    return jnp.dot(first_op, second_op, preferred_element_type=F32)


def dot_high(first_op, second_op):
    return jnp.dot(first_op, second_op, precision=HIGH, preferred_element_type=F32)


def dot_rows(first_op, second_op):
    return lax.dot_general(
        first_op, second_op, (((0,), (0,)), ((), ())), precision=HIGH, preferred_element_type=F32
    )


def dot_lanes(first_op, second_op, precision=None):
    return lax.dot_general(
        first_op,
        second_op,
        (((1,), (1,)), ((), ())),
        precision=precision,
        preferred_element_type=F32,
    )


def fold(wide):
    half = wide.shape[0] // 2
    return jnp.concatenate([wide[:half], wide[half:]], axis=1)


def unfold(packed):
    return jnp.concatenate([packed[:, :RANK], packed[:, RANK:]], axis=0)


def identity():
    row = lax.broadcasted_iota(jnp.int32, (RANK, RANK), 0)
    col = lax.broadcasted_iota(jnp.int32, (RANK, RANK), 1)
    return jnp.where(row == col, 1.0, 0.0).astype(F32)


def spd_inverse(gram):
    row = lax.broadcasted_iota(jnp.int32, (RANK, LANES), 0)

    def eliminate(_, both):
        cols = [jnp.broadcast_to(both[:, j : j + 1], (RANK, LANES)) for j in range(8)]
        for j in range(8):
            over = 1.0 / cols[j][j : j + 1, :]
            here = row == j
            pivot_row = both[j : j + 1, :] * over
            both = jnp.where(here, pivot_row, both - cols[j] * pivot_row)
            for later in range(j + 1, 8):
                entry = cols[later][j : j + 1, :] * over
                cols[later] = jnp.where(here, entry, cols[later] - cols[j] * entry)
        both = jnp.concatenate([both[8:], both[:8]], axis=0)
        return pltpu.roll(both, LANES - 8, 1)

    both = jnp.concatenate([gram, identity()], axis=1)
    return lax.fori_loop(0, RANK // 8, eliminate, both)[:, :RANK]


def threshold_of(sums, weight):
    count = jnp.sum(sums[0:1, :], axis=1, keepdims=True)
    total = jnp.sum(sums[1:2, :], axis=1, keepdims=True)
    penalty = count / (4.0 * total + 1e-06)
    return penalty, weight / penalty


def gram_blocks(stacked):
    return dot_lanes(stacked, stacked)


def sum_blocks(wide):
    rows = wide[0:64] + (wide[64:128] + wide[128:192])
    return rows[:, 0:64] + (rows[:, 64:128] + rows[:, 128:192])


def left_stack(left):
    first, second = split(left, 2)
    return jnp.concatenate([first, first, second, second], axis=1)


def low_rank(stacked_left, first, second):
    return dot(stacked_left, jnp.concatenate([first, second, first, second], axis=0))


def block_at(half, group):
    return pl.ds(pl.multiple_of(half * 2048 + group * BLOCK, BLOCK), BLOCK)


def join_chunks(chunks, half, group):
    return jnp.concatenate([chunks[half, group, i] for i in range(4)], axis=1)


def factorize(weight, *refs):
    readings, missing, left_in, right_in, seen, clipped, left_out, right_out, sums_out = refs[:9]
    (miss, high, low_part, scaled, right_start, left_start, acc, gram_sum, sums, x_gram, x_gram_in, x_sums,
     x_sums_in, gram_own, gram_core, gram_send, gram_in, gram_total, gram_twin, partial, from_core, arrived, right_mid, sems, load_sems) = refs[9:]
    used = [0]
    tm = lax.axis_index("tm")
    me = lax.axis_index("sys")
    core = me % 2
    y = (me // 2) % 4
    z = me // 8
    ring = (2, 1, 3)

    def at_sys(z_pos, y_pos, core_pos):
        return {"sys": (z_pos * 4 + y_pos) * 2 + core_pos}

    twin = at_sys(z, y, 1 - core)
    x_dev = {k: {"tm": (tm + k) % 4} for k in ring}
    plane = {
        (ky, kz): at_sys((z + kz) % 4, (y + ky) % 4, core)
        for ky in range(4) for kz in range(4) if ky or kz
    }

    def send(src, dst, device):
        index = used[0]
        used[0] += 1
        copy = pltpu.make_async_remote_copy(
            src_ref=src, dst_ref=dst, send_sem=sems.at[0, index], recv_sem=sems.at[1, index],
            device_id=device, device_id_type=MESH,
        )
        copy.start()
        return copy

    def load(src, dst, index):
        copy = pltpu.make_async_copy(src, dst, load_sems.at[index])
        copy.start()
        return copy

    small_loads = [load(right_in, right_start, 0), load(left_in, left_start, 1)]
    blocks = [slice(j * BLOCK, (j + 1) * BLOCK) for j in range(8)]
    loads = [
        (load(readings.at[:, at], seen.at[:, at], 2 + 2 * j), load(missing.at[:, at], miss.at[:, at], 3 + 2 * j))
        for j, at in enumerate(blocks)
    ]
    barrier = pltpu.get_barrier_semaphore()
    everyone = list(x_dev.values()) + [twin] + list(plane.values())
    for device in everyone:
        pl.semaphore_signal(barrier, inc=1, device_id=device, device_id_type=MESH)
    for copy in small_loads:
        copy.wait()

    def send_gram(turn, gram):
        x_gram[turn] = fold(gram)
        return [send(x_gram.at[turn], x_gram_in.at[turn, k - 1], x_dev[k]) for k in ring]

    def send_sums(turn):
        return [send(x_sums.at[turn], x_sums_in.at[turn, k - 1], x_dev[k]) for k in ring]

    def finish_gram(turn, copies):
        for copy in copies:
            copy.wait()
        total = (x_gram[turn] + x_gram_in[turn, 0]) + (x_gram_in[turn, 1] + x_gram_in[turn, 2])
        return spd_inverse(unfold(total) + identity())

    def finish_sums(turn, copies):
        for copy in copies:
            copy.wait()
        return (x_sums[turn] + x_sums_in[turn, 0]) + (x_sums_in[turn, 1] + x_sums_in[turn, 2])

    stacked_left = left_stack(left_start[...].T)
    acc[...] = jnp.zeros_like(acc)
    gram_sum[...] = jnp.zeros_like(gram_sum)
    sums[...] = jnp.zeros_like(sums)
    for at in blocks:
        stacked = jnp.concatenate(split(right_start[:, at], 3), axis=0)
        gram_sum[...] += gram_blocks(stacked)
    for at, copies in zip(blocks, loads):
        right_a, right_b, right_c = split(right_start[:, at], 3)
        low = low_rank(stacked_left, right_a, right_b)
        for copy in copies:
            copy.wait()
        observed = miss[:, at] == 0
        value = seen[:, at]
        seen[:, at] = jnp.where(observed, value, ABSENT)
        target_a, target_b = split(jnp.where(observed, value, low), 2)
        high[:, at] = target_a
        low_part[:, at] = target_b
        acc[...] += dot_lanes(target_a, jnp.concatenate([right_a, right_b, right_c], axis=0))
        acc[:, :LANES] += dot_lanes(target_b, jnp.concatenate([right_a, right_b], axis=0))
        count = jnp.sum(jnp.where(observed, 1.0, 0.0), axis=0, keepdims=True)
        total = jnp.sum(jnp.where(observed, jnp.abs(value), 0.0), axis=0, keepdims=True)
        for piece in range(BLOCK // LANES):
            lanes = slice(piece * LANES, (piece + 1) * LANES)
            sums[0:1, :] += count[:, lanes]
            sums[1:2, :] += total[:, lanes]
    pl.semaphore_wait(barrier, len(everyone))
    gram_copies = send_gram(0, sum_blocks(gram_sum[...]))
    x_sums[0, 0:128, :] = fold(acc[:, :RANK] + acc[:, RANK : 2 * RANK] + acc[:, 2 * RANK :])
    x_sums[0, 128:136, :] = sums[...]
    sum_copies = send_sums(0)
    inverse = finish_gram(0, gram_copies)
    summed = finish_sums(0, sum_copies)
    left = dot_high(unfold(summed[0:128]), inverse)
    left_out[0] = left.T

    def update_right(turn, left, stacked, extra, products, finish, target, send_order):
        gram_own[turn] = fold(sum_blocks(gram_blocks(stacked)))
        theirs = pl.ds(pl.multiple_of(16 * (1 - core), 16), 16)
        ours = pl.ds(pl.multiple_of(16 * core, 16), 16)
        gram_copy = send(gram_own.at[turn, theirs], gram_core.at[turn], twin)
        order = (2, 1, 3, 0)
        core_copies = {}
        for ky in order:
            group = (y + ky) % 4
            products(1 - core, group)
            core_copies[ky] = send(partial.at[turn, 1 - core, group], from_core.at[turn, ky], twin)
        gram_copy.wait()
        gram_send[turn, 0:16, :] = gram_own[turn, ours, :] + gram_core[turn]
        gram_send[turn, 16:24, :] = extra
        gram_copies = [
            send(gram_send.at[turn], gram_in.at[turn, 4 * ky + kz - 1], plane[ky, kz])
            for ky in order for kz in order if ky or kz
        ]
        scattered = []
        for ky in order:
            group = (y + ky) % 4
            products(core, group)
            core_copies[ky].wait()
            partial[turn, core, group] += from_core[turn, ky]
            for kz in order:
                if ky or kz:
                    scattered.append(
                        send(partial.at[turn, core, group, (z + kz) % 4], arrived.at[turn, 4 * ky + kz - 1],
                             plane[ky, kz])
                    )
        for copy in gram_copies:
            copy.wait()
        total = gram_send[turn]
        for k in range(0, 15, 3):
            total += (gram_in[turn, k] + gram_in[turn, k + 1]) + gram_in[turn, k + 2]
        gram_total[turn] = total
        send(gram_total.at[turn], gram_twin.at[turn], twin).wait()
        other = gram_twin[turn]
        folded = jnp.concatenate(
            [jnp.where(core == 0, total[0:16], other[0:16]), jnp.where(core == 0, other[0:16], total[0:16])], axis=0
        )
        inverse = spd_inverse(unfold(folded) + identity())
        finish(total[16:24] + other[16:24])
        for copy in scattered:
            copy.wait()
        total = partial[turn, core, y, z]
        for k in range(0, 15, 3):
            total += (arrived[turn, k] + arrived[turn, k + 1]) + arrived[turn, k + 2]
        target[core, y, z] = dot_high(inverse, total)
        mine = target.at[core, y, z]
        gather = {}
        for ky in send_order:
            for kz in send_order:
                if ky or kz:
                    gather[ky, kz] = send(mine, mine, plane[ky, kz])
        near_first = (0, 1, 3, 2)
        to_twin = {}
        for ky in near_first:
            for kz in near_first:
                if ky or kz:
                    gather[ky, kz].wait()
            group = (y + 4 - ky) % 4
            here = target.at[core, group]
            to_twin[ky] = send(here, here, twin)
            yield core, group
        for ky in near_first:
            to_twin[ky].wait()
        for ky in near_first:
            yield 1 - core, (y + 4 - ky) % 4

    def finish_first(total):
        sums_out[...] = total

    stack_a, stack_b, stack_c = split(left.T, 3)
    stacked_two = jnp.concatenate([stack_a, stack_b], axis=0)
    stacked_three = jnp.concatenate([stack_a, stack_b, stack_c], axis=0)

    def products_first(half, group):
        at = block_at(half, group)
        wide = dot(stacked_three, high[:, at])
        small = dot(stacked_two, low_part[:, at])
        value = wide[0:64] + (wide[64:128] + (wide[128:192] + (small[0:64] + small[64:128])))
        for i in range(4):
            partial[0, half, group, i] = value[:, i * LANES : (i + 1) * LANES]

    stacked_left = left_stack(left)
    acc[...] = jnp.zeros_like(acc)
    gram_sum[...] = jnp.zeros_like(gram_sum)
    near = (0, 1, 3, 2)
    far = (2, 1, 3, 0)
    seen_blocks = 0
    waiting = []
    gram_copies = None

    def middle(half, group):
        _, bound = threshold_of(sums_out[...], weight)
        at = block_at(half, group)
        right_a, right_b = split(join_chunks(right_mid, half, group), 2)
        low = low_rank(stacked_left, right_a, right_b)
        value = seen[:, at]
        inside = jnp.maximum(jnp.minimum(value - low, bound), -bound)
        inside = jnp.where(value < 0.5 * ABSENT, inside, 0.0)
        clipped[:, at] = inside
        ratio = (inside * (1.0 / bound)).astype(BF16)
        scaled[:, at] = ratio
        acc[:, :LANES] += dot_lanes(ratio, jnp.concatenate([right_a, right_b], axis=0))

    for half, group in update_right(
        0, left, stacked_three, summed[128:136], products_first, finish_first, right_mid, near
    ):
        stacked = jnp.concatenate(split(join_chunks(right_mid, half, group), 3), axis=0)
        gram_sum[...] += gram_blocks(stacked)
        seen_blocks += 1
        if seen_blocks <= 4:
            middle(half, group)
        else:
            waiting.append((half, group))
    gram_copies = send_gram(1, sum_blocks(gram_sum[...]))
    for half, group in waiting:
        middle(half, group)
    _, bound = threshold_of(sums_out[...], weight)
    scale = (5.0 / 3.0) * bound
    x_sums[1, 0:128, :] = fold((acc[:, :RANK] + acc[:, RANK : 2 * RANK]) * scale)
    x_sums[1, 128:136, :] = jnp.zeros((8, LANES), F32)
    sum_copies = send_sums(1)
    inverse = finish_gram(1, gram_copies)
    summed = finish_sums(1, sum_copies)
    before = left
    left = before + dot_high(unfold(summed[0:128]) - before, inverse)
    left_out[1] = left.T
    mix_a, mix_b, mix_c = split(dot_rows(left, before), 3)
    mixed = jnp.concatenate([mix_a, mix_a, mix_b, mix_c], axis=1)
    stacked_all = jnp.concatenate(split(left.T, 3), axis=0)
    stacked_last = stacked_all[0:128]

    def products_last(half, group):
        at = block_at(half, group)
        wide = dot(stacked_last, scaled[:, at])
        right_a, right_b = split(join_chunks(right_mid, half, group), 2)
        value = dot(mixed, jnp.concatenate([right_a, right_b, right_a, right_a], axis=0))
        value += (wide[0:64] + wide[64:128]) * scale
        for i in range(4):
            partial[1, half, group, i] = value[:, i * LANES : (i + 1) * LANES]

    for _ in update_right(
        1, left, stacked_all, jnp.zeros((8, LANES), F32), products_last, lambda total: None, right_out, far
    ):
        pass


def last_pass(weight, seen, clipped, left, right, sums, sparse, dual, right_t, left_t, sparse_v, dual_v, right_v, sems):
    used = []

    def store(src, dst):
        copy = pltpu.make_async_copy(src, dst, sems.at[len(used)])
        copy.start()
        used.append(copy)

    store(left.at[1], left_t)
    penalty, bound = threshold_of(sums[...], weight)
    penalty = 1.5 * penalty
    bound = bound / 1.5
    stacked_left = left_stack(left[1].T)
    for block in range(8):
        at = slice(block * BLOCK, (block + 1) * BLOCK)
        cols = join_chunks(right, block // 4, block % 4)
        right_v[:, at] = cols
        store(right_v.at[:, at], right_t.at[:, at])
        right_a, right_b = split(cols, 2)
        low = low_rank(stacked_left, right_a, right_b)
        value = seen[:, at]
        present = value < 0.5 * ABSENT
        shifted = value - low + clipped[:, at] * (1.0 / 1.5)
        inside = jnp.maximum(jnp.minimum(shifted, bound), -bound)
        sparse_v[:, at] = jnp.where(present, shifted - inside, 0.0)
        store(sparse_v.at[:, at], sparse.at[:, at])
        dual_v[:, at] = jnp.where(present, inside * penalty, 0.0)
        store(dual_v.at[:, at], dual.at[:, at])
    for copy in used:
        copy.wait()


def params(limit, **more):
    return pltpu.CompilerParams(vmem_limit_bytes=limit * MIB, **more)


def on_device(weight, readings, missing, left_init, right_init):
    rows, times = readings.shape
    shape = jax.ShapeDtypeStruct
    full = shape((rows, times), F32)
    dma = pltpu.SemaphoreType.DMA
    in_vmem = pl.BlockSpec(memory_space=VMEM)
    in_hbm = pl.BlockSpec(memory_space=pltpu.HBM)
    chunked = (2, 4, 4, RANK, LANES)
    seen, clipped, left, right, sums = pl.pallas_call(
        functools.partial(factorize, weight),
        out_shape=[full, full, shape((2, RANK, rows), F32), shape(chunked, F32), shape((8, LANES), F32)],
        in_specs=[in_hbm] * 4,
        out_specs=[in_vmem] * 5,
        scratch_shapes=[
            VMEM((rows, times), jnp.int32),
            VMEM((rows, times), BF16),
            VMEM((rows, times), BF16),
            VMEM((rows, times), BF16),
            VMEM((RANK, times), F32),
            VMEM((RANK, rows), F32),
            VMEM((rows, 3 * RANK), F32),
            VMEM((3 * RANK, 3 * RANK), F32),
            VMEM((8, LANES), F32),
            VMEM((2, 32, LANES), F32),
            VMEM((2, 3, 32, LANES), F32),
            VMEM((2, 136, LANES), F32),
            VMEM((2, 3, 136, LANES), F32),
            VMEM((2, 32, LANES), F32),
            VMEM((2, 16, LANES), F32),
            VMEM((2, 24, LANES), F32),
            VMEM((2, 15, 24, LANES), F32),
            VMEM((2, 24, LANES), F32),
            VMEM((2, 24, LANES), F32),
            VMEM((2,) + chunked, F32),
            VMEM((2, 4, 4, RANK, LANES), F32),
            VMEM((2, 15, RANK, LANES), F32),
            VMEM(chunked, F32),
            dma((2, 122)),
            dma((18,)),
        ],
        compiler_params=params(40, collective_id=0, has_side_effects=True),
    )(*(pltpu.with_memory_space_constraint(arg, pltpu.HBM) for arg in (readings, missing, left_init.T, right_init.T)))
    sparse, dual, right_t, left_t = pl.pallas_call(
        functools.partial(last_pass, weight),
        out_shape=[full, full, shape((RANK, times), F32), shape((RANK, rows), F32)],
        in_specs=[in_vmem] * 5,
        out_specs=[in_hbm] * 4,
        scratch_shapes=[VMEM((rows, times), F32), VMEM((rows, times), F32), VMEM((RANK, times), F32), dma((25,))],
        compiler_params=params(24),
    )(seen, clipped, left, right, sums)
    return left_t.T, right_t.T, sparse, dual


def solution(mesh):
    weight = 1.0 / math.sqrt(max(8192, 16384))
    in_specs = (P("sys", "tm"), P("sys", "tm"), P("sys", None), P("tm", None))
    out_specs = (P("sys", None), P("tm", None), P("sys", "tm"), P("sys", "tm"))
    return jax.shard_map(
        functools.partial(on_device, weight), mesh=mesh, in_specs=in_specs, out_specs=out_specs, check_vma=False
    )
```

```python
import functools
import math

import jax
import jax.numpy as jnp
from jax import lax
from jax.experimental import pallas as pl
from jax.experimental.pallas import tpu as pltpu
from jax.sharding import PartitionSpec as P

F32 = jnp.float32
BF16 = jnp.bfloat16
HIGH = lax.Precision.HIGHEST
MESH = pl.DeviceIdType.MESH
VMEM = pltpu.VMEM
RANK = 64
LANES = 128
ABSENT = 1e30
BLOCK = 512
MIB = 1 << 20
PARTS = 2
WIDE = 1024
NEAR = (0, 1, 3, 2)
FAR = (2, 1, 3, 0)
FIRST_ORDER = FAR


def split(value, parts):
    pieces = []
    for part in range(parts):
        piece = value.astype(BF16)
        pieces.append(piece)
        if part + 1 < parts:
            value = value - piece.astype(F32)
    return pieces


def dot(first_op, second_op):
    return jnp.dot(first_op, second_op, preferred_element_type=F32)


def dot_high(first_op, second_op):
    return jnp.dot(first_op, second_op, precision=HIGH, preferred_element_type=F32)


def dot_rows(first_op, second_op):
    return lax.dot_general(
        first_op, second_op, (((0,), (0,)), ((), ())), precision=HIGH, preferred_element_type=F32
    )


def dot_lanes(first_op, second_op, precision=None):
    return lax.dot_general(
        first_op,
        second_op,
        (((1,), (1,)), ((), ())),
        precision=precision,
        preferred_element_type=F32,
    )


def fold(wide):
    half = wide.shape[0] // 2
    return jnp.concatenate([wide[:half], wide[half:]], axis=1)


def unfold(packed):
    return jnp.concatenate([packed[:, :RANK], packed[:, RANK:]], axis=0)


def identity():
    row = lax.broadcasted_iota(jnp.int32, (RANK, RANK), 0)
    col = lax.broadcasted_iota(jnp.int32, (RANK, RANK), 1)
    return jnp.where(row == col, 1.0, 0.0).astype(F32)


def spd_inverse(gram):
    row = lax.broadcasted_iota(jnp.int32, (RANK, LANES), 0)

    def eliminate(_, both):
        cols = [jnp.broadcast_to(both[:, j : j + 1], (RANK, LANES)) for j in range(8)]
        for j in range(8):
            over = 1.0 / cols[j][j : j + 1, :]
            here = row == j
            pivot_row = both[j : j + 1, :] * over
            both = jnp.where(here, pivot_row, both - cols[j] * pivot_row)
            for later in range(j + 1, 8):
                entry = cols[later][j : j + 1, :] * over
                cols[later] = jnp.where(here, entry, cols[later] - cols[j] * entry)
        both = jnp.concatenate([both[8:], both[:8]], axis=0)
        return pltpu.roll(both, LANES - 8, 1)

    both = jnp.concatenate([gram, identity()], axis=1)
    return lax.fori_loop(0, RANK // 8, eliminate, both)[:, :RANK]


def threshold_of(sums, weight):
    count = jnp.sum(sums[0:1, :], axis=1, keepdims=True)
    total = jnp.sum(sums[1:2, :], axis=1, keepdims=True)
    penalty = count / (4.0 * total + 1e-06)
    return penalty, weight / penalty


def gram_blocks(stacked):
    return dot_lanes(stacked, stacked)


def sum_blocks(wide):
    rows = wide[0:64] + (wide[64:128] + wide[128:192])
    return rows[:, 0:64] + (rows[:, 64:128] + rows[:, 128:192])


def solver(inverse):
    first, second, third = split(inverse, 3)
    large = jnp.concatenate([first, first, second, second], axis=1)
    small = jnp.concatenate([first, third], axis=1)

    def solve(cols):
        col_a, col_b, col_c = split(cols, 3)
        fine = dot(small, jnp.concatenate([col_c, col_a], axis=0))
        return fine + dot(large, jnp.concatenate([col_a, col_b, col_a, col_b], axis=0))

    return solve


def left_stack(left):
    first, second = split(left, 2)
    return jnp.concatenate([first, first, second, second], axis=1)


def low_rank(stacked_left, first, second):
    return dot(stacked_left, jnp.concatenate([first, second, first, second], axis=0))


def block_at(half, group):
    return pl.ds(pl.multiple_of(half * 2048 + group * BLOCK, BLOCK), BLOCK)


def join_chunks(chunks, half, group):
    return jnp.concatenate([chunks[half, group, i] for i in range(4)], axis=1)


def factorize(weight, *refs):
    readings, missing, left_in, right_in, seen, clipped, left_out, right_out, sums_out, inverse_out = refs[:10]
    (miss, high, low_part, scaled, right_start, left_start, acc, gram_sum, sums, x_gram, x_gram_in, x_sums,
     x_sums_in, gram_send, gram_core, gram_y, gram_z, partial, from_core, arrived, right_mid, right_solved, sems, load_sems) = refs[10:]
    used = [0]
    tm = lax.axis_index("tm")
    me = lax.axis_index("sys")
    core = me % 2
    y = (me // 2) % 4
    z = me // 8
    ring = (2, 1, 3)

    def at_sys(z_pos, y_pos, core_pos):
        return {"sys": (z_pos * 4 + y_pos) * 2 + core_pos}

    twin = at_sys(z, y, 1 - core)
    y_dev = {k: at_sys(z, (y + k) % 4, core) for k in ring}
    z_dev = {k: at_sys((z + k) % 4, y, core) for k in ring}
    x_dev = {k: {"tm": (tm + k) % 4} for k in ring}
    plane = {
        (ky, kz): at_sys((z + kz) % 4, (y + ky) % 4, core)
        for ky in range(4) for kz in range(4) if ky or kz
    }

    def send(src, dst, device):
        index = used[0]
        used[0] += 1
        copy = pltpu.make_async_remote_copy(
            src_ref=src, dst_ref=dst, send_sem=sems.at[0, index], recv_sem=sems.at[1, index],
            device_id=device, device_id_type=MESH,
        )
        copy.start()
        return copy

    def load(src, dst, index):
        copy = pltpu.make_async_copy(src, dst, load_sems.at[index])
        copy.start()
        return copy

    small_loads = [load(right_in, right_start, 0), load(left_in, left_start, 1)]
    blocks = [slice(j * BLOCK, (j + 1) * BLOCK) for j in range(8)]
    loads = [
        (load(readings.at[:, at], seen.at[:, at], 2 + 2 * j), load(missing.at[:, at], miss.at[:, at], 3 + 2 * j))
        for j, at in enumerate(blocks)
    ]
    barrier = pltpu.get_barrier_semaphore()
    everyone = list(x_dev.values()) + [twin] + list(plane.values())
    for device in everyone:
        pl.semaphore_signal(barrier, inc=1, device_id=device, device_id_type=MESH)
    for copy in small_loads:
        copy.wait()

    def send_gram(turn, gram):
        x_gram[turn] = fold(gram)
        return [send(x_gram.at[turn], x_gram_in.at[turn, k - 1], x_dev[k]) for k in ring]

    def send_sums(turn):
        return [send(x_sums.at[turn], x_sums_in.at[turn, k - 1], x_dev[k]) for k in ring]

    def finish_gram(turn, copies):
        for copy in copies:
            copy.wait()
        total = (x_gram[turn] + x_gram_in[turn, 0]) + (x_gram_in[turn, 1] + x_gram_in[turn, 2])
        return spd_inverse(unfold(total) + identity())

    def finish_sums(turn, copies):
        for copy in copies:
            copy.wait()
        return (x_sums[turn] + x_sums_in[turn, 0]) + (x_sums_in[turn, 1] + x_sums_in[turn, 2])

    stacked_left = left_stack(left_start[...].T)
    acc[...] = jnp.zeros_like(acc)
    gram_sum[...] = jnp.zeros_like(gram_sum)
    sums[...] = jnp.zeros_like(sums)
    for at in blocks:
        stacked = jnp.concatenate(split(right_start[:, at], 3), axis=0)
        gram_sum[...] += gram_blocks(stacked)
    for block, (at, copies) in enumerate(zip(blocks, loads)):
        if block == 4:
            pl.semaphore_wait(barrier, len(everyone))
            gram_copies = send_gram(0, sum_blocks(gram_sum[...]))
        right_a, right_b, right_c = split(right_start[:, at], 3)
        low = low_rank(stacked_left, right_a, right_b)
        for copy in copies:
            copy.wait()
        observed = miss[:, at] == 0
        value = seen[:, at]
        seen[:, at] = jnp.where(observed, value, ABSENT)
        target_a, target_b = split(jnp.where(observed, value, low), 2)
        high[:, at] = target_a
        low_part[:, at] = target_b
        acc[...] += dot_lanes(target_a, jnp.concatenate([right_a, right_b, right_c], axis=0))
        acc[:, :LANES] += dot_lanes(target_b, jnp.concatenate([right_a, right_b], axis=0))
        count = jnp.sum(jnp.where(observed, 1.0, 0.0), axis=0, keepdims=True)
        total = jnp.sum(jnp.where(observed, jnp.abs(value), 0.0), axis=0, keepdims=True)
        for piece in range(BLOCK // LANES):
            lanes = slice(piece * LANES, (piece + 1) * LANES)
            sums[0:1, :] += count[:, lanes]
            sums[1:2, :] += total[:, lanes]
    x_sums[0, 0:128, :] = fold(acc[:, :RANK] + acc[:, RANK : 2 * RANK] + acc[:, 2 * RANK :])
    x_sums[0, 128:136, :] = sums[...]
    sum_copies = send_sums(0)
    inverse = finish_gram(0, gram_copies)
    summed = finish_sums(0, sum_copies)
    left = dot_high(unfold(summed[0:128]), inverse)
    left_out[0] = left.T

    def update_right(turn, stacked, extra, products, finish, target, send_order):
        gram_send[turn, 0, 0:32, :] = fold(sum_blocks(gram_blocks(stacked)))
        gram_send[turn, 0, 32:40, :] = extra
        gram_copy = send(gram_send.at[turn, 0], gram_core.at[turn], twin)
        order = (2, 1, 3, 0)
        core_copies = {}
        for ky in order:
            group = (y + ky) % 4
            products(1 - core, group)
            core_copies[ky] = send(partial.at[turn, 1 - core, group], from_core.at[turn, ky], twin)
        gram_copy.wait()
        gram_send[turn, 1] = gram_send[turn, 0] + gram_core[turn]
        y_copies = [send(gram_send.at[turn, 1], gram_y.at[turn, k - 1], y_dev[k]) for k in ring]
        parts = [slice(i * RANK // PARTS, (i + 1) * RANK // PARTS) for i in range(PARTS)]

        def scatter(ky, part):
            group = (y + ky) % 4
            return [
                send(partial.at[turn, core, group, (z + kz) % 4, part], arrived.at[turn, 4 * ky + kz - 1, part],
                     plane[ky, kz])
                for kz in order if ky or kz
            ]

        scattered = [[] for _ in parts]
        for ky in order:
            group = (y + ky) % 4
            products(core, group)
            core_copies[ky].wait()
            partial[turn, core, group] += from_core[turn, ky]
            scattered[0] += scatter(ky, parts[0])
        for part, copies in zip(parts[1:], scattered[1:]):
            for ky in order:
                copies += scatter(ky, part)
        for copy in y_copies:
            copy.wait()
        gram_send[turn, 2] = (gram_send[turn, 1] + gram_y[turn, 0]) + (gram_y[turn, 1] + gram_y[turn, 2])
        z_copies = [send(gram_send.at[turn, 2], gram_z.at[turn, k - 1], z_dev[k]) for k in ring]
        mine = target.at[core, y, z]
        gather = {(ky, kz): [] for ky in range(4) for kz in range(4)}
        for part, copies in zip(parts, scattered):
            for copy in copies:
                copy.wait()
            total = partial[turn, core, y, z, part]
            for k in range(0, 15, 3):
                total += (arrived[turn, k, part] + arrived[turn, k + 1, part]) + arrived[turn, k + 2, part]
            target[core, y, z, part] = total
            for ky in send_order:
                for kz in send_order:
                    if ky or kz:
                        gather[ky, kz].append(send(mine.at[part], mine.at[part], plane[ky, kz]))
        for copy in z_copies:
            copy.wait()
        grams = (gram_send[turn, 2] + gram_z[turn, 0]) + (gram_z[turn, 1] + gram_z[turn, 2])
        finish(spd_inverse(unfold(grams[0:32]) + identity()), grams[32:40])
        near_first = (0, 1, 3, 2)
        to_twin = {}
        for ky in near_first:
            for kz in near_first:
                for copy in gather[ky, kz]:
                    copy.wait()
            group = (y + 4 - ky) % 4
            here = target.at[core, group]
            to_twin[ky] = send(here, here, twin)
            yield core, group
        for ky in near_first:
            to_twin[ky].wait()

    def finish_first(inverse, total):
        sums_out[...] = total
        inverse_out[0] = inverse

    def finish_last(inverse, total):
        inverse_out[1] = inverse

    stack_a, stack_b, stack_c = split(left.T, 3)
    stacked_two = jnp.concatenate([stack_a, stack_b], axis=0)
    stacked_three = jnp.concatenate([stack_a, stack_b, stack_c], axis=0)

    def products_first(half, group):
        at = block_at(half, group)
        wide = dot(stacked_three, high[:, at])
        small = dot(stacked_two, low_part[:, at])
        value = wide[0:64] + (wide[64:128] + (wide[128:192] + (small[0:64] + small[64:128])))
        for i in range(4):
            partial[0, half, group, i] = value[:, i * LANES : (i + 1) * LANES]

    stacked_left = left_stack(left)
    acc[...] = jnp.zeros_like(acc)
    gram_sum[...] = jnp.zeros_like(gram_sum)

    def middle(at, bound):
        right_a, right_b = split(right_solved[:, at], 2)
        low = low_rank(stacked_left, right_a, right_b)
        value = seen[:, at]
        inside = jnp.maximum(jnp.minimum(value - low, bound), -bound)
        inside = jnp.where(value < 0.5 * ABSENT, inside, 0.0)
        clipped[:, at] = inside
        ratio = (inside * (1.0 / bound)).astype(BF16)
        scaled[:, at] = ratio
        acc[:, :LANES] += dot_lanes(ratio, jnp.concatenate([right_a, right_b], axis=0))

    def solve_block(half, group, solve):
        at = block_at(half, group)
        cols = solve(join_chunks(right_mid, half, group))
        right_solved[:, at] = cols
        gram_sum[...] += gram_blocks(jnp.concatenate(split(cols, 3), axis=0))
        return at

    for half, group in update_right(
        0, stacked_three, summed[128:136], products_first, finish_first, right_mid, FIRST_ORDER
    ):
        at = solve_block(half, group, solver(inverse_out[0]))
        middle(at, threshold_of(sums_out[...], weight)[1])
    solve = solver(inverse_out[0])
    for group in range(4):
        solve_block(1 - core, group, solve)
    gram_copies = send_gram(1, sum_blocks(gram_sum[...]))
    for wide in range(2048 // WIDE):
        at = pl.ds(pl.multiple_of((1 - core) * 2048 + wide * WIDE, WIDE), WIDE)
        middle(at, threshold_of(sums_out[...], weight)[1])
    _, bound = threshold_of(sums_out[...], weight)
    scale = (5.0 / 3.0) * bound
    x_sums[1, 0:128, :] = fold((acc[:, :RANK] + acc[:, RANK : 2 * RANK]) * scale)
    x_sums[1, 128:136, :] = jnp.zeros((8, LANES), F32)
    sum_copies = send_sums(1)
    inverse = finish_gram(1, gram_copies)
    summed = finish_sums(1, sum_copies)
    before = left
    left = before + dot_high(unfold(summed[0:128]) - before, inverse)
    left_out[1] = left.T
    mix_a, mix_b, mix_c = split(dot_rows(left, before), 3)
    mixed = jnp.concatenate([mix_a, mix_a, mix_b, mix_c], axis=1)
    stacked_all = jnp.concatenate(split(left.T, 3), axis=0)
    stacked_last = stacked_all[0:128]

    def products_last(half, group):
        at = block_at(half, group)
        wide = dot(stacked_last, scaled[:, at])
        right_a, right_b = split(right_solved[:, at], 2)
        value = dot(mixed, jnp.concatenate([right_a, right_b, right_a, right_a], axis=0))
        value += (wide[0:64] + wide[64:128]) * scale
        for i in range(4):
            partial[1, half, group, i] = value[:, i * LANES : (i + 1) * LANES]

    for _ in update_right(
        1, stacked_all, jnp.zeros((8, LANES), F32), products_last, finish_last, right_out, FAR
    ):
        pass


def last_pass(weight, seen, clipped, left, right, sums, inverse, sparse, dual, right_t, left_t, sparse_v, dual_v, right_v,
              sems):
    used = []

    def store(src, dst):
        copy = pltpu.make_async_copy(src, dst, sems.at[len(used)])
        copy.start()
        used.append(copy)

    store(left.at[1], left_t)
    penalty, bound = threshold_of(sums[...], weight)
    penalty = 1.5 * penalty
    bound = bound / 1.5
    stacked_left = left_stack(left[1].T)
    solve = solver(inverse[1])
    for block in range(8):
        at = slice(block * BLOCK, (block + 1) * BLOCK)
        cols = solve(join_chunks(right, block // 4, block % 4))
        right_v[:, at] = cols
        store(right_v.at[:, at], right_t.at[:, at])
        right_a, right_b = split(cols, 2)
        low = low_rank(stacked_left, right_a, right_b)
        value = seen[:, at]
        present = value < 0.5 * ABSENT
        shifted = value - low + clipped[:, at] * (1.0 / 1.5)
        inside = jnp.maximum(jnp.minimum(shifted, bound), -bound)
        sparse_v[:, at] = jnp.where(present, shifted - inside, 0.0)
        store(sparse_v.at[:, at], sparse.at[:, at])
        dual_v[:, at] = jnp.where(present, inside * penalty, 0.0)
        store(dual_v.at[:, at], dual.at[:, at])
    for copy in used:
        copy.wait()


def params(limit, **more):
    return pltpu.CompilerParams(vmem_limit_bytes=limit * MIB, **more)


def on_device(weight, readings, missing, left_init, right_init):
    rows, times = readings.shape
    shape = jax.ShapeDtypeStruct
    full = shape((rows, times), F32)
    dma = pltpu.SemaphoreType.DMA
    in_vmem = pl.BlockSpec(memory_space=VMEM)
    in_hbm = pl.BlockSpec(memory_space=pltpu.HBM)
    chunked = (2, 4, 4, RANK, LANES)
    seen, clipped, left, right, sums, inverse = pl.pallas_call(
        functools.partial(factorize, weight),
        out_shape=[full, full, shape((2, RANK, rows), F32), shape(chunked, F32), shape((8, LANES), F32),
                   shape((2, RANK, RANK), F32)],
        in_specs=[in_hbm] * 4,
        out_specs=[in_vmem] * 6,
        scratch_shapes=[
            VMEM((rows, times), jnp.int32),
            VMEM((rows, times), BF16),
            VMEM((rows, times), BF16),
            VMEM((rows, times), BF16),
            VMEM((RANK, times), F32),
            VMEM((RANK, rows), F32),
            VMEM((rows, 3 * RANK), F32),
            VMEM((3 * RANK, 3 * RANK), F32),
            VMEM((8, LANES), F32),
            VMEM((2, 32, LANES), F32),
            VMEM((2, 3, 32, LANES), F32),
            VMEM((2, 136, LANES), F32),
            VMEM((2, 3, 136, LANES), F32),
            VMEM((2, 3, 40, LANES), F32),
            VMEM((2, 40, LANES), F32),
            VMEM((2, 3, 40, LANES), F32),
            VMEM((2, 3, 40, LANES), F32),
            VMEM((2,) + chunked, F32),
            VMEM((2, 4, 4, RANK, LANES), F32),
            VMEM((2, 15, RANK, LANES), F32),
            VMEM(chunked, F32),
            VMEM((RANK, times), F32),
            dma((2, 2 * (21 + 30 * PARTS))),
            dma((18,)),
        ],
        compiler_params=params(40, collective_id=0, has_side_effects=True),
    )(*(pltpu.with_memory_space_constraint(arg, pltpu.HBM) for arg in (readings, missing, left_init.T, right_init.T)))
    sparse, dual, right_t, left_t = pl.pallas_call(
        functools.partial(last_pass, weight),
        out_shape=[full, full, shape((RANK, times), F32), shape((RANK, rows), F32)],
        in_specs=[in_vmem] * 6,
        out_specs=[in_hbm] * 4,
        scratch_shapes=[VMEM((rows, times), F32), VMEM((rows, times), F32), VMEM((RANK, times), F32), dma((25,))],
        compiler_params=params(24),
    )(seen, clipped, left, right, sums, inverse)
    return left_t.T, right_t.T, sparse, dual


def solution(mesh):
    weight = 1.0 / math.sqrt(max(8192, 16384))
    in_specs = (P("sys", "tm"), P("sys", "tm"), P("sys", None), P("tm", None))
    out_specs = (P("sys", None), P("tm", None), P("sys", "tm"), P("sys", "tm"))
    return jax.shard_map(
        functools.partial(on_device, weight), mesh=mesh, in_specs=in_specs, out_specs=out_specs, check_vma=False
    )
```

```python
import functools
import math

import jax
import jax.numpy as jnp
from jax import lax
from jax.experimental import pallas as pl
from jax.experimental.pallas import tpu as pltpu
from jax.sharding import PartitionSpec as P

F32 = jnp.float32
BF16 = jnp.bfloat16
HIGH = lax.Precision.HIGHEST
MESH = pl.DeviceIdType.MESH
VMEM = pltpu.VMEM
RANK = 64
LANES = 128
ABSENT = 1e30
BLOCK = 512
MIB = 1 << 20
PARTS = 2
WIDE = 1024
MEET = 6


def split(value, parts):
    pieces = []
    for part in range(parts):
        piece = value.astype(BF16)
        pieces.append(piece)
        if part + 1 < parts:
            value = value - piece.astype(F32)
    return pieces


def dot(first_op, second_op):
    return jnp.dot(first_op, second_op, preferred_element_type=F32)


def dot_high(first_op, second_op):
    return jnp.dot(first_op, second_op, precision=HIGH, preferred_element_type=F32)


def dot_rows(first_op, second_op):
    return lax.dot_general(
        first_op, second_op, (((0,), (0,)), ((), ())), precision=HIGH, preferred_element_type=F32
    )


def dot_lanes(first_op, second_op, precision=None):
    return lax.dot_general(
        first_op,
        second_op,
        (((1,), (1,)), ((), ())),
        precision=precision,
        preferred_element_type=F32,
    )


def fold(wide):
    half = wide.shape[0] // 2
    return jnp.concatenate([wide[:half], wide[half:]], axis=1)


def unfold(packed):
    return jnp.concatenate([packed[:, :RANK], packed[:, RANK:]], axis=0)


def identity():
    row = lax.broadcasted_iota(jnp.int32, (RANK, RANK), 0)
    col = lax.broadcasted_iota(jnp.int32, (RANK, RANK), 1)
    return jnp.where(row == col, 1.0, 0.0).astype(F32)


def spd_inverse(gram):
    row = lax.broadcasted_iota(jnp.int32, (RANK, LANES), 0)

    def eliminate(_, both):
        cols = [jnp.broadcast_to(both[:, j : j + 1], (RANK, LANES)) for j in range(8)]
        for j in range(8):
            over = 1.0 / cols[j][j : j + 1, :]
            here = row == j
            pivot_row = both[j : j + 1, :] * over
            both = jnp.where(here, pivot_row, both - cols[j] * pivot_row)
            for later in range(j + 1, 8):
                entry = cols[later][j : j + 1, :] * over
                cols[later] = jnp.where(here, entry, cols[later] - cols[j] * entry)
        both = jnp.concatenate([both[8:], both[:8]], axis=0)
        return pltpu.roll(both, LANES - 8, 1)

    both = jnp.concatenate([gram, identity()], axis=1)
    return lax.fori_loop(0, RANK // 8, eliminate, both)[:, :RANK]


def threshold_of(sums, weight):
    count = jnp.sum(sums[0:1, :], axis=1, keepdims=True)
    total = jnp.sum(sums[1:2, :], axis=1, keepdims=True)
    penalty = count / (4.0 * total + 1e-06)
    return penalty, weight / penalty


def gram_blocks(stacked):
    return dot_lanes(stacked, stacked)


def sum_blocks(wide):
    rows = wide[0:64] + (wide[64:128] + wide[128:192])
    return rows[:, 0:64] + (rows[:, 64:128] + rows[:, 128:192])


def solver(inverse):
    first, second, third = split(inverse, 3)
    large = jnp.concatenate([first, first, second, second], axis=1)
    small = jnp.concatenate([first, third], axis=1)

    def solve(cols):
        col_a, col_b, col_c = split(cols, 3)
        fine = dot(small, jnp.concatenate([col_c, col_a], axis=0))
        return fine + dot(large, jnp.concatenate([col_a, col_b, col_a, col_b], axis=0))

    return solve


def left_stack(left):
    first, second = split(left, 2)
    return jnp.concatenate([first, first, second, second], axis=1)


def low_rank(stacked_left, first, second):
    return dot(stacked_left, jnp.concatenate([first, second, first, second], axis=0))


def block_at(half, group):
    return pl.ds(pl.multiple_of(half * 2048 + group * BLOCK, BLOCK), BLOCK)


def join_chunks(chunks, half, group):
    return jnp.concatenate([chunks[half, group, i] for i in range(4)], axis=1)


def factorize(weight, *refs):
    readings, missing, left_in, right_in, seen, clipped, left_out, right_out, sums_out, inverse_out = refs[:10]
    (miss, high, low_part, scaled, right_start, left_start, acc, gram_sum, sums, x_gram, x_gram_in, x_sums,
     x_sums_in, gram_send, gram_core, gram_y, gram_z, partial, from_core, arrived, right_mid, right_solved, gram_half, sems, load_sems) = refs[10:]
    used = [0]
    tm = lax.axis_index("tm")
    me = lax.axis_index("sys")
    core = me % 2
    y = (me // 2) % 4
    z = me // 8
    ring = (2, 1, 3)

    def at_sys(z_pos, y_pos, core_pos):
        return {"sys": (z_pos * 4 + y_pos) * 2 + core_pos}

    twin = at_sys(z, y, 1 - core)
    y_dev = {k: at_sys(z, (y + k) % 4, core) for k in ring}
    z_dev = {k: at_sys((z + k) % 4, y, core) for k in ring}
    x_dev = {k: {"tm": (tm + k) % 4} for k in ring}
    plane = {
        (ky, kz): at_sys((z + kz) % 4, (y + ky) % 4, core)
        for ky in range(4) for kz in range(4) if ky or kz
    }

    def send(src, dst, device):
        index = used[0]
        used[0] += 1
        copy = pltpu.make_async_remote_copy(
            src_ref=src, dst_ref=dst, send_sem=sems.at[0, index], recv_sem=sems.at[1, index],
            device_id=device, device_id_type=MESH,
        )
        copy.start()
        return copy

    def load(src, dst, index):
        copy = pltpu.make_async_copy(src, dst, load_sems.at[index])
        copy.start()
        return copy

    barrier = pltpu.get_barrier_semaphore()
    everyone = list(x_dev.values()) + [twin] + list(plane.values())
    for device in everyone:
        pl.semaphore_signal(barrier, inc=1, device_id=device, device_id_type=MESH)
    small_loads = [load(right_in, right_start, 0), load(left_in, left_start, 1)]
    blocks = [slice(j * BLOCK, (j + 1) * BLOCK) for j in range(8)]
    loads = [
        (load(readings.at[:, at], seen.at[:, at], 2 + 2 * j), load(missing.at[:, at], miss.at[:, at], 3 + 2 * j))
        for j, at in enumerate(blocks)
    ]
    for copy in small_loads:
        copy.wait()

    def send_gram(turn, folded):
        x_gram[turn] = folded
        return [send(x_gram.at[turn], x_gram_in.at[turn, k - 1], x_dev[k]) for k in ring]

    def send_sums(turn):
        return [send(x_sums.at[turn], x_sums_in.at[turn, k - 1], x_dev[k]) for k in ring]

    def finish_gram(turn, copies):
        for copy in copies:
            copy.wait()
        total = (x_gram[turn] + x_gram_in[turn, 0]) + (x_gram_in[turn, 1] + x_gram_in[turn, 2])
        return spd_inverse(unfold(total) + identity())

    def finish_sums(turn, copies):
        for copy in copies:
            copy.wait()
        return (x_sums[turn] + x_sums_in[turn, 0]) + (x_sums_in[turn, 1] + x_sums_in[turn, 2])

    stacked_left = left_stack(left_start[...].T)
    acc[...] = jnp.zeros_like(acc)
    gram_sum[...] = jnp.zeros_like(gram_sum)
    sums[...] = jnp.zeros_like(sums)
    for at in blocks:
        stacked = jnp.concatenate(split(right_start[:, at], 3), axis=0)
        gram_sum[...] += gram_blocks(stacked)
    for block, (at, copies) in enumerate(zip(blocks, loads)):
        if block == MEET:
            pl.semaphore_wait(barrier, len(everyone))
            gram_copies = send_gram(0, fold(sum_blocks(gram_sum[...])))
        right_a, right_b, right_c = split(right_start[:, at], 3)
        low = low_rank(stacked_left, right_a, right_b)
        for copy in copies:
            copy.wait()
        observed = miss[:, at] == 0
        value = seen[:, at]
        seen[:, at] = jnp.where(observed, value, ABSENT)
        target_a, target_b = split(jnp.where(observed, value, low), 2)
        high[:, at] = target_a
        low_part[:, at] = target_b
        acc[...] += dot_lanes(target_a, jnp.concatenate([right_a, right_b, right_c], axis=0))
        acc[:, :LANES] += dot_lanes(target_b, jnp.concatenate([right_a, right_b], axis=0))
        count = jnp.sum(jnp.where(observed, 1.0, 0.0), axis=0, keepdims=True)
        total = jnp.sum(jnp.where(observed, jnp.abs(value), 0.0), axis=0, keepdims=True)
        for piece in range(BLOCK // LANES):
            lanes = slice(piece * LANES, (piece + 1) * LANES)
            sums[0:1, :] += count[:, lanes]
            sums[1:2, :] += total[:, lanes]
    x_sums[0, 0:128, :] = fold(acc[:, :RANK] + acc[:, RANK : 2 * RANK] + acc[:, 2 * RANK :])
    x_sums[0, 128:136, :] = sums[...]
    sum_copies = send_sums(0)
    inverse = finish_gram(0, gram_copies)
    summed = finish_sums(0, sum_copies)
    left = dot_high(unfold(summed[0:128]), inverse)
    left_out[0] = left.T

    def update_right(turn, stacked, extra, products, finish, target, ready, between):
        gram_send[turn, 0, 0:32, :] = fold(sum_blocks(gram_blocks(stacked)))
        gram_send[turn, 0, 32:40, :] = extra
        gram_copy = send(gram_send.at[turn, 0], gram_core.at[turn], twin)
        order = (2, 1, 3, 0)
        core_copies = {}
        for ky in order:
            group = (y + ky) % 4
            products(1 - core, group)
            core_copies[ky] = send(partial.at[turn, 1 - core, group], from_core.at[turn, ky], twin)
        gram_copy.wait()
        gram_send[turn, 1] = gram_send[turn, 0] + gram_core[turn]
        y_copies = [send(gram_send.at[turn, 1], gram_y.at[turn, k - 1], y_dev[k]) for k in ring]
        parts = [slice(i * RANK // PARTS, (i + 1) * RANK // PARTS) for i in range(PARTS)]

        def scatter(ky, part):
            group = (y + ky) % 4
            return [
                send(partial.at[turn, core, group, (z + kz) % 4, part], arrived.at[turn, 4 * ky + kz - 1, part],
                     plane[ky, kz])
                for kz in order if ky or kz
            ]

        scattered = [[] for _ in parts]
        for ky in order:
            group = (y + ky) % 4
            products(core, group)
            core_copies[ky].wait()
            partial[turn, core, group] += from_core[turn, ky]
            scattered[0] += scatter(ky, parts[0])
        for part, copies in zip(parts[1:], scattered[1:]):
            for ky in order:
                copies += scatter(ky, part)
        for copy in y_copies:
            copy.wait()
        gram_send[turn, 2] = (gram_send[turn, 1] + gram_y[turn, 0]) + (gram_y[turn, 1] + gram_y[turn, 2])
        z_copies = [send(gram_send.at[turn, 2], gram_z.at[turn, k - 1], z_dev[k]) for k in ring]
        mine = target.at[core, y, z]
        gather = {(ky, kz): [] for ky in range(4) for kz in range(4)}
        for part, copies in zip(parts, scattered):
            for copy in copies:
                copy.wait()
            total = partial[turn, core, y, z, part]
            for k in range(0, 15, 3):
                total += (arrived[turn, k, part] + arrived[turn, k + 1, part]) + arrived[turn, k + 2, part]
            target[core, y, z, part] = total
            for ky in order:
                for kz in order:
                    if ky or kz:
                        gather[ky, kz].append(send(mine.at[part], mine.at[part], plane[ky, kz]))
        for copy in z_copies:
            copy.wait()
        grams = (gram_send[turn, 2] + gram_z[turn, 0]) + (gram_z[turn, 1] + gram_z[turn, 2])
        finish(spd_inverse(unfold(grams[0:32]) + identity()), grams[32:40])
        near_first = (0, 1, 3, 2)
        to_twin = {}
        for ky in near_first:
            for kz in near_first:
                for copy in gather[ky, kz]:
                    copy.wait()
            here = ready((y + 4 - ky) % 4)
            to_twin[ky] = send(here, here, twin)
        between()
        for ky in near_first:
            to_twin[ky].wait()

    def finish_first(inverse, total):
        sums_out[...] = total
        inverse_out[0] = inverse

    def finish_last(inverse, total):
        inverse_out[1] = inverse

    stack_a, stack_b, stack_c = split(left.T, 3)
    stacked_two = jnp.concatenate([stack_a, stack_b], axis=0)
    stacked_three = jnp.concatenate([stack_a, stack_b, stack_c], axis=0)

    def products_first(half, group):
        at = block_at(half, group)
        wide = dot(stacked_three, high[:, at])
        small = dot(stacked_two, low_part[:, at])
        value = wide[0:64] + (wide[64:128] + (wide[128:192] + (small[0:64] + small[64:128])))
        for i in range(4):
            partial[0, half, group, i] = value[:, i * LANES : (i + 1) * LANES]

    stacked_left = left_stack(left)
    acc[...] = jnp.zeros_like(acc)
    gram_sum[...] = jnp.zeros_like(gram_sum)

    def middle(at, bound):
        right_a, right_b = split(right_solved[:, at], 2)
        low = low_rank(stacked_left, right_a, right_b)
        value = seen[:, at]
        inside = jnp.maximum(jnp.minimum(value - low, bound), -bound)
        inside = jnp.where(value < 0.5 * ABSENT, inside, 0.0)
        clipped[:, at] = inside
        ratio = (inside * (1.0 / bound)).astype(BF16)
        scaled[:, at] = ratio
        acc[:, :LANES] += dot_lanes(ratio, jnp.concatenate([right_a, right_b], axis=0))

    def middle_half(half):
        for wide in range(2048 // WIDE):
            at = pl.ds(pl.multiple_of(half * 2048 + wide * WIDE, WIDE), WIDE)
            middle(at, threshold_of(sums_out[...], weight)[1])

    def solve_block(group):
        at = block_at(core, group)
        cols = solver(inverse_out[0])(join_chunks(right_mid, core, group))
        right_solved[:, at] = cols
        gram_sum[...] += gram_blocks(jnp.concatenate(split(cols, 3), axis=0))
        return right_solved.at[:, at]

    gram_copies = []

    def own_half():
        gram_half[0] = fold(sum_blocks(gram_sum[...]))
        copy = send(gram_half.at[0], gram_half.at[1], twin)
        middle_half(core)
        copy.wait()
        gram_copies.extend(send_gram(1, gram_half[0] + gram_half[1]))

    update_right(
        0, stacked_three, summed[128:136], products_first, finish_first, right_mid, solve_block, own_half
    )
    middle_half(1 - core)
    _, bound = threshold_of(sums_out[...], weight)
    scale = (5.0 / 3.0) * bound
    x_sums[1, 0:128, :] = fold((acc[:, :RANK] + acc[:, RANK : 2 * RANK]) * scale)
    x_sums[1, 128:136, :] = jnp.zeros((8, LANES), F32)
    sum_copies = send_sums(1)
    inverse = finish_gram(1, gram_copies)
    summed = finish_sums(1, sum_copies)
    before = left
    left = before + dot_high(unfold(summed[0:128]) - before, inverse)
    left_out[1] = left.T
    mix_a, mix_b, mix_c = split(dot_rows(left, before), 3)
    mixed = jnp.concatenate([mix_a, mix_a, mix_b, mix_c], axis=1)
    stacked_all = jnp.concatenate(split(left.T, 3), axis=0)
    stacked_last = stacked_all[0:128]

    def products_last(half, group):
        at = block_at(half, group)
        wide = dot(stacked_last, scaled[:, at])
        right_a, right_b = split(right_solved[:, at], 2)
        value = dot(mixed, jnp.concatenate([right_a, right_b, right_a, right_a], axis=0))
        value += (wide[0:64] + wide[64:128]) * scale
        for i in range(4):
            partial[1, half, group, i] = value[:, i * LANES : (i + 1) * LANES]

    update_right(
        1, stacked_all, jnp.zeros((8, LANES), F32), products_last, finish_last, right_out,
        lambda group: right_out.at[core, group], lambda: None,
    )


def last_pass(weight, seen, clipped, left, right, sums, inverse, sparse, dual, right_t, left_t, sparse_v, dual_v, right_v,
              sems):
    used = []

    def store(src, dst):
        copy = pltpu.make_async_copy(src, dst, sems.at[len(used)])
        copy.start()
        used.append(copy)

    store(left.at[1], left_t)
    penalty, bound = threshold_of(sums[...], weight)
    penalty = 1.5 * penalty
    bound = bound / 1.5
    stacked_left = left_stack(left[1].T)
    solve = solver(inverse[1])
    for block in range(8):
        at = slice(block * BLOCK, (block + 1) * BLOCK)
        cols = solve(join_chunks(right, block // 4, block % 4))
        right_v[:, at] = cols
        store(right_v.at[:, at], right_t.at[:, at])
        right_a, right_b = split(cols, 2)
        low = low_rank(stacked_left, right_a, right_b)
        value = seen[:, at]
        present = value < 0.5 * ABSENT
        shifted = value - low + clipped[:, at] * (1.0 / 1.5)
        inside = jnp.maximum(jnp.minimum(shifted, bound), -bound)
        sparse_v[:, at] = jnp.where(present, shifted - inside, 0.0)
        store(sparse_v.at[:, at], sparse.at[:, at])
        dual_v[:, at] = jnp.where(present, inside * penalty, 0.0)
        store(dual_v.at[:, at], dual.at[:, at])
    for copy in used:
        copy.wait()


def params(limit, **more):
    return pltpu.CompilerParams(vmem_limit_bytes=limit * MIB, **more)


def on_device(weight, readings, missing, left_init, right_init):
    rows, times = readings.shape
    shape = jax.ShapeDtypeStruct
    full = shape((rows, times), F32)
    dma = pltpu.SemaphoreType.DMA
    in_vmem = pl.BlockSpec(memory_space=VMEM)
    in_hbm = pl.BlockSpec(memory_space=pltpu.HBM)
    chunked = (2, 4, 4, RANK, LANES)
    seen, clipped, left, right, sums, inverse = pl.pallas_call(
        functools.partial(factorize, weight),
        out_shape=[full, full, shape((2, RANK, rows), F32), shape(chunked, F32), shape((8, LANES), F32),
                   shape((2, RANK, RANK), F32)],
        in_specs=[in_hbm] * 4,
        out_specs=[in_vmem] * 6,
        scratch_shapes=[
            VMEM((rows, times), jnp.int32),
            VMEM((rows, times), BF16),
            VMEM((rows, times), BF16),
            VMEM((rows, times), BF16),
            VMEM((RANK, times), F32),
            VMEM((RANK, rows), F32),
            VMEM((rows, 3 * RANK), F32),
            VMEM((3 * RANK, 3 * RANK), F32),
            VMEM((8, LANES), F32),
            VMEM((2, 32, LANES), F32),
            VMEM((2, 3, 32, LANES), F32),
            VMEM((2, 136, LANES), F32),
            VMEM((2, 3, 136, LANES), F32),
            VMEM((2, 3, 40, LANES), F32),
            VMEM((2, 40, LANES), F32),
            VMEM((2, 3, 40, LANES), F32),
            VMEM((2, 3, 40, LANES), F32),
            VMEM((2,) + chunked, F32),
            VMEM((2, 4, 4, RANK, LANES), F32),
            VMEM((2, 15, RANK, LANES), F32),
            VMEM(chunked, F32),
            VMEM((RANK, times), F32),
            VMEM((2, 32, LANES), F32),
            dma((2, 43 + 60 * PARTS)),
            dma((18,)),
        ],
        compiler_params=params(40, collective_id=0, has_side_effects=True),
    )(*(pltpu.with_memory_space_constraint(arg, pltpu.HBM) for arg in (readings, missing, left_init.T, right_init.T)))
    sparse, dual, right_t, left_t = pl.pallas_call(
        functools.partial(last_pass, weight),
        out_shape=[full, full, shape((RANK, times), F32), shape((RANK, rows), F32)],
        in_specs=[in_vmem] * 6,
        out_specs=[in_hbm] * 4,
        scratch_shapes=[VMEM((rows, times), F32), VMEM((rows, times), F32), VMEM((RANK, times), F32), dma((25,))],
        compiler_params=params(24),
    )(seen, clipped, left, right, sums, inverse)
    return left_t.T, right_t.T, sparse, dual


def solution(mesh):
    weight = 1.0 / math.sqrt(max(8192, 16384))
    in_specs = (P("sys", "tm"), P("sys", "tm"), P("sys", None), P("tm", None))
    out_specs = (P("sys", None), P("tm", None), P("sys", "tm"), P("sys", "tm"))
    return jax.shard_map(
        functools.partial(on_device, weight), mesh=mesh, in_specs=in_specs, out_specs=out_specs, check_vma=False
    )
```

```python
import functools
import math

import jax
import jax.numpy as jnp
from jax import lax
from jax.experimental import pallas as pl
from jax.experimental.pallas import tpu as pltpu
from jax.sharding import PartitionSpec as P

F32 = jnp.float32
BF16 = jnp.bfloat16
HIGH = lax.Precision.HIGHEST
MESH = pl.DeviceIdType.MESH
VMEM = pltpu.VMEM
RANK = 64
LANES = 128
ABSENT = 1e30
BLOCK = 512
MIB = 1 << 20
PARTS = 2
WIDE = 1024
MEET = 5


def split(value, parts):
    pieces = []
    for part in range(parts):
        piece = value.astype(BF16)
        pieces.append(piece)
        if part + 1 < parts:
            value = value - piece.astype(F32)
    return pieces


def dot(first_op, second_op):
    return jnp.dot(first_op, second_op, preferred_element_type=F32)


def dot_high(first_op, second_op):
    return jnp.dot(first_op, second_op, precision=HIGH, preferred_element_type=F32)


def dot_rows(first_op, second_op):
    return lax.dot_general(
        first_op, second_op, (((0,), (0,)), ((), ())), precision=HIGH, preferred_element_type=F32
    )


def dot_lanes(first_op, second_op, precision=None):
    return lax.dot_general(
        first_op,
        second_op,
        (((1,), (1,)), ((), ())),
        precision=precision,
        preferred_element_type=F32,
    )


def fold(wide):
    half = wide.shape[0] // 2
    return jnp.concatenate([wide[:half], wide[half:]], axis=1)


def unfold(packed):
    return jnp.concatenate([packed[:, :RANK], packed[:, RANK:]], axis=0)


def identity():
    row = lax.broadcasted_iota(jnp.int32, (RANK, RANK), 0)
    col = lax.broadcasted_iota(jnp.int32, (RANK, RANK), 1)
    return jnp.where(row == col, 1.0, 0.0).astype(F32)


def spd_inverse(gram):
    row = lax.broadcasted_iota(jnp.int32, (RANK, LANES), 0)

    def eliminate(_, both):
        cols = [jnp.broadcast_to(both[:, j : j + 1], (RANK, LANES)) for j in range(8)]
        for j in range(8):
            over = 1.0 / cols[j][j : j + 1, :]
            here = row == j
            pivot_row = both[j : j + 1, :] * over
            both = jnp.where(here, pivot_row, both - cols[j] * pivot_row)
            for later in range(j + 1, 8):
                entry = cols[later][j : j + 1, :] * over
                cols[later] = jnp.where(here, entry, cols[later] - cols[j] * entry)
        both = jnp.concatenate([both[8:], both[:8]], axis=0)
        return pltpu.roll(both, LANES - 8, 1)

    both = jnp.concatenate([gram, identity()], axis=1)
    return lax.fori_loop(0, RANK // 8, eliminate, both)[:, :RANK]


def threshold_of(sums, weight):
    count = jnp.sum(sums[0:1, :], axis=1, keepdims=True)
    total = jnp.sum(sums[1:2, :], axis=1, keepdims=True)
    penalty = count / (4.0 * total + 1e-06)
    return penalty, weight / penalty


def gram_blocks(stacked):
    return dot_lanes(stacked, stacked)


def sum_blocks(wide):
    rows = wide[0:64] + (wide[64:128] + wide[128:192])
    return rows[:, 0:64] + (rows[:, 64:128] + rows[:, 128:192])


def solver(inverse):
    first, second, third = split(inverse, 3)
    large = jnp.concatenate([first, first, second, second], axis=1)
    small = jnp.concatenate([first, third], axis=1)

    def solve(cols):
        col_a, col_b, col_c = split(cols, 3)
        fine = dot(small, jnp.concatenate([col_c, col_a], axis=0))
        return fine + dot(large, jnp.concatenate([col_a, col_b, col_a, col_b], axis=0))

    return solve


def left_stack(left):
    first, second = split(left, 2)
    return jnp.concatenate([first, first, second, second], axis=1)


def low_rank(stacked_left, first, second):
    return dot(stacked_left, jnp.concatenate([first, second, first, second], axis=0))


def block_at(half, group):
    return pl.ds(pl.multiple_of(half * 2048 + group * BLOCK, BLOCK), BLOCK)


def join_chunks(chunks, half, group):
    return jnp.concatenate([chunks[half, group, i] for i in range(4)], axis=1)


def factorize(weight, *refs):
    readings, missing, left_in, right_in, seen, clipped, left_out, right_out, sums_out, inverse_out = refs[:10]
    (miss, high, low_part, scaled, right_start, left_start, acc, gram_sum, sums, x_gram, x_gram_in, x_sums,
     x_sums_in, gram_send, gram_core, gram_y, gram_z, partial, from_core, arrived, right_mid, right_solved, gram_half, sems, load_sems) = refs[10:]
    used = [0]
    tm = lax.axis_index("tm")
    me = lax.axis_index("sys")
    core = me % 2
    y = (me // 2) % 4
    z = me // 8
    ring = (2, 1, 3)

    def at_sys(z_pos, y_pos, core_pos):
        return {"sys": (z_pos * 4 + y_pos) * 2 + core_pos}

    twin = at_sys(z, y, 1 - core)
    y_dev = {k: at_sys(z, (y + k) % 4, core) for k in ring}
    z_dev = {k: at_sys((z + k) % 4, y, core) for k in ring}
    x_dev = {k: {"tm": (tm + k) % 4} for k in ring}
    plane = {
        (ky, kz): at_sys((z + kz) % 4, (y + ky) % 4, core)
        for ky in range(4) for kz in range(4) if ky or kz
    }

    def send(src, dst, device):
        index = used[0]
        used[0] += 1
        copy = pltpu.make_async_remote_copy(
            src_ref=src, dst_ref=dst, send_sem=sems.at[0, index], recv_sem=sems.at[1, index],
            device_id=device, device_id_type=MESH,
        )
        copy.start()
        return copy

    def load(src, dst, index):
        copy = pltpu.make_async_copy(src, dst, load_sems.at[index])
        copy.start()
        return copy

    barrier = pltpu.get_barrier_semaphore()
    everyone = list(x_dev.values()) + [twin] + list(plane.values())
    for device in everyone:
        pl.semaphore_signal(barrier, inc=1, device_id=device, device_id_type=MESH)
    small_loads = [load(right_in, right_start, 0), load(left_in, left_start, 1)]
    blocks = [slice(j * BLOCK, (j + 1) * BLOCK) for j in range(8)]
    loads = [
        (load(readings.at[:, at], seen.at[:, at], 2 + 2 * j), load(missing.at[:, at], miss.at[:, at], 3 + 2 * j))
        for j, at in enumerate(blocks)
    ]
    for copy in small_loads:
        copy.wait()

    def send_gram(turn, folded):
        x_gram[turn] = folded
        return [send(x_gram.at[turn], x_gram_in.at[turn, k - 1], x_dev[k]) for k in ring]

    def send_sums(turn):
        return [send(x_sums.at[turn], x_sums_in.at[turn, k - 1], x_dev[k]) for k in ring]

    def finish_gram(turn, copies):
        for copy in copies:
            copy.wait()
        total = (x_gram[turn] + x_gram_in[turn, 0]) + (x_gram_in[turn, 1] + x_gram_in[turn, 2])
        return spd_inverse(unfold(total) + identity())

    def finish_sums(turn, copies):
        for copy in copies:
            copy.wait()
        return (x_sums[turn] + x_sums_in[turn, 0]) + (x_sums_in[turn, 1] + x_sums_in[turn, 2])

    stacked_left = left_stack(left_start[...].T)
    acc[...] = jnp.zeros_like(acc)
    gram_sum[...] = jnp.zeros_like(gram_sum)
    sums[...] = jnp.zeros_like(sums)
    for at in blocks:
        stacked = jnp.concatenate(split(right_start[:, at], 3), axis=0)
        gram_sum[...] += gram_blocks(stacked)
    for block, (at, copies) in enumerate(zip(blocks, loads)):
        if block == MEET:
            pl.semaphore_wait(barrier, len(everyone))
            gram_copies = send_gram(0, fold(sum_blocks(gram_sum[...])))
        right_a, right_b, right_c = split(right_start[:, at], 3)
        low = low_rank(stacked_left, right_a, right_b)
        for copy in copies:
            copy.wait()
        observed = miss[:, at] == 0
        value = seen[:, at]
        seen[:, at] = jnp.where(observed, value, ABSENT)
        target_a, target_b = split(jnp.where(observed, value, low), 2)
        high[:, at] = target_a
        low_part[:, at] = target_b
        acc[...] += dot_lanes(target_a, jnp.concatenate([right_a, right_b, right_c], axis=0))
        acc[:, :LANES] += dot_lanes(target_b, jnp.concatenate([right_a, right_b], axis=0))
        count = jnp.sum(jnp.where(observed, 1.0, 0.0), axis=0, keepdims=True)
        total = jnp.sum(jnp.where(observed, jnp.abs(value), 0.0), axis=0, keepdims=True)
        for piece in range(BLOCK // LANES):
            lanes = slice(piece * LANES, (piece + 1) * LANES)
            sums[0:1, :] += count[:, lanes]
            sums[1:2, :] += total[:, lanes]
    x_sums[0, 0:128, :] = fold(acc[:, :RANK] + acc[:, RANK : 2 * RANK] + acc[:, 2 * RANK :])
    x_sums[0, 128:136, :] = sums[...]
    sum_copies = send_sums(0)
    inverse = finish_gram(0, gram_copies)
    summed = finish_sums(0, sum_copies)
    left = dot_high(unfold(summed[0:128]), inverse)
    left_out[0] = left.T

    def update_right(turn, stacked, extra, products, finish, target, ready, between):
        gram_send[turn, 0, 0:32, :] = fold(sum_blocks(gram_blocks(stacked)))
        gram_send[turn, 0, 32:40, :] = extra
        gram_copy = send(gram_send.at[turn, 0], gram_core.at[turn], twin)
        order = (2, 1, 3, 0)
        core_copies = {}
        for ky in order:
            group = (y + ky) % 4
            products(1 - core, group)
            core_copies[ky] = send(partial.at[turn, 1 - core, group], from_core.at[turn, ky], twin)
        gram_copy.wait()
        gram_send[turn, 1] = gram_send[turn, 0] + gram_core[turn]
        y_copies = [send(gram_send.at[turn, 1], gram_y.at[turn, k - 1], y_dev[k]) for k in ring]
        parts = [slice(i * RANK // PARTS, (i + 1) * RANK // PARTS) for i in range(PARTS)]

        def scatter(ky, part):
            group = (y + ky) % 4
            return [
                send(partial.at[turn, core, group, (z + kz) % 4, part], arrived.at[turn, 4 * ky + kz - 1, part],
                     plane[ky, kz])
                for kz in order if ky or kz
            ]

        scattered = [[] for _ in parts]
        for ky in order:
            group = (y + ky) % 4
            products(core, group)
            core_copies[ky].wait()
            partial[turn, core, group] += from_core[turn, ky]
            scattered[0] += scatter(ky, parts[0])
        for part, copies in zip(parts[1:], scattered[1:]):
            for ky in order:
                copies += scatter(ky, part)
        for copy in y_copies:
            copy.wait()
        gram_send[turn, 2] = (gram_send[turn, 1] + gram_y[turn, 0]) + (gram_y[turn, 1] + gram_y[turn, 2])
        z_copies = [send(gram_send.at[turn, 2], gram_z.at[turn, k - 1], z_dev[k]) for k in ring]
        mine = target.at[core, y, z]
        gather = {(ky, kz): [] for ky in range(4) for kz in range(4)}
        for part, copies in zip(parts, scattered):
            for copy in copies:
                copy.wait()
            total = partial[turn, core, y, z, part]
            for k in range(0, 15, 3):
                total += (arrived[turn, k, part] + arrived[turn, k + 1, part]) + arrived[turn, k + 2, part]
            target[core, y, z, part] = total
            for ky in order:
                for kz in order:
                    if ky or kz:
                        gather[ky, kz].append(send(mine.at[part], mine.at[part], plane[ky, kz]))
        for copy in z_copies:
            copy.wait()
        grams = (gram_send[turn, 2] + gram_z[turn, 0]) + (gram_z[turn, 1] + gram_z[turn, 2])
        finish(spd_inverse(unfold(grams[0:32]) + identity()), grams[32:40])
        near_first = (0, 1, 3, 2)
        to_twin = {}
        for ky in near_first:
            for kz in near_first:
                for copy in gather[ky, kz]:
                    copy.wait()
            here = ready((y + 4 - ky) % 4)
            to_twin[ky] = send(here, here, twin)
        between()
        for ky in near_first:
            to_twin[ky].wait()

    def finish_first(inverse, total):
        sums_out[...] = total
        inverse_out[0] = inverse

    def finish_last(inverse, total):
        inverse_out[1] = inverse

    stack_a, stack_b, stack_c = split(left.T, 3)
    stacked_two = jnp.concatenate([stack_a, stack_b], axis=0)
    stacked_three = jnp.concatenate([stack_a, stack_b, stack_c], axis=0)

    def products_first(half, group):
        at = block_at(half, group)
        wide = dot(stacked_three, high[:, at])
        small = dot(stacked_two, low_part[:, at])
        value = wide[0:64] + (wide[64:128] + (wide[128:192] + (small[0:64] + small[64:128])))
        for i in range(4):
            partial[0, half, group, i] = value[:, i * LANES : (i + 1) * LANES]

    stacked_left = left_stack(left)
    acc[...] = jnp.zeros_like(acc)
    gram_sum[...] = jnp.zeros_like(gram_sum)

    def middle(at, bound):
        right_a, right_b = split(right_solved[:, at], 2)
        low = low_rank(stacked_left, right_a, right_b)
        value = seen[:, at]
        inside = jnp.maximum(jnp.minimum(value - low, bound), -bound)
        inside = jnp.where(value < 0.5 * ABSENT, inside, 0.0)
        clipped[:, at] = inside
        ratio = (inside * (1.0 / bound)).astype(BF16)
        scaled[:, at] = ratio
        acc[:, :LANES] += dot_lanes(ratio, jnp.concatenate([right_a, right_b], axis=0))

    def middle_half(half):
        for wide in range(2048 // WIDE):
            at = pl.ds(pl.multiple_of(half * 2048 + wide * WIDE, WIDE), WIDE)
            middle(at, threshold_of(sums_out[...], weight)[1])

    def solve_block(group):
        at = block_at(core, group)
        cols = solver(inverse_out[0])(join_chunks(right_mid, core, group))
        right_solved[:, at] = cols
        gram_sum[...] += gram_blocks(jnp.concatenate(split(cols, 3), axis=0))
        return right_solved.at[:, at]

    gram_copies = []

    def own_half():
        gram_half[0] = fold(sum_blocks(gram_sum[...]))
        copy = send(gram_half.at[0], gram_half.at[1], twin)
        middle_half(core)
        copy.wait()
        gram_copies.extend(send_gram(1, gram_half[0] + gram_half[1]))

    update_right(
        0, stacked_three, summed[128:136], products_first, finish_first, right_mid, solve_block, own_half
    )
    middle_half(1 - core)
    _, bound = threshold_of(sums_out[...], weight)
    scale = (5.0 / 3.0) * bound
    x_sums[1, 0:128, :] = fold((acc[:, :RANK] + acc[:, RANK : 2 * RANK]) * scale)
    x_sums[1, 128:136, :] = jnp.zeros((8, LANES), F32)
    sum_copies = send_sums(1)
    inverse = finish_gram(1, gram_copies)
    summed = finish_sums(1, sum_copies)
    before = left
    left = before + dot_high(unfold(summed[0:128]) - before, inverse)
    left_out[1] = left.T
    mix_a, mix_b, mix_c = split(dot_rows(left, before), 3)
    mixed = jnp.concatenate([mix_a, mix_a, mix_b, mix_c], axis=1)
    stacked_all = jnp.concatenate(split(left.T, 3), axis=0)
    stacked_last = stacked_all[0:128]

    def products_last(half, group):
        at = block_at(half, group)
        wide = dot(stacked_last, scaled[:, at])
        right_a, right_b = split(right_solved[:, at], 2)
        value = dot(mixed, jnp.concatenate([right_a, right_b, right_a, right_a], axis=0))
        value += (wide[0:64] + wide[64:128]) * scale
        for i in range(4):
            partial[1, half, group, i] = value[:, i * LANES : (i + 1) * LANES]

    update_right(
        1, stacked_all, jnp.zeros((8, LANES), F32), products_last, finish_last, right_out,
        lambda group: right_out.at[core, group], lambda: None,
    )


def last_pass(weight, seen, clipped, left, right, sums, inverse, sparse, dual, right_t, left_t, sparse_v, dual_v, right_v,
              sems):
    used = []

    def store(src, dst):
        copy = pltpu.make_async_copy(src, dst, sems.at[len(used)])
        copy.start()
        used.append(copy)

    store(left.at[1], left_t)
    penalty, bound = threshold_of(sums[...], weight)
    penalty = 1.5 * penalty
    bound = bound / 1.5
    stacked_left = left_stack(left[1].T)
    solve = solver(inverse[1])
    for block in range(8):
        at = slice(block * BLOCK, (block + 1) * BLOCK)
        right_v[:, at] = solve(join_chunks(right, block // 4, block % 4))
        store(right_v.at[:, at], right_t.at[:, at])
    for block in range(8):
        at = slice(block * BLOCK, (block + 1) * BLOCK)
        right_a, right_b = split(right_v[:, at], 2)
        low = low_rank(stacked_left, right_a, right_b)
        value = seen[:, at]
        present = value < 0.5 * ABSENT
        shifted = value - low + clipped[:, at] * (1.0 / 1.5)
        inside = jnp.maximum(jnp.minimum(shifted, bound), -bound)
        sparse_v[:, at] = jnp.where(present, shifted - inside, 0.0)
        store(sparse_v.at[:, at], sparse.at[:, at])
        dual_v[:, at] = jnp.where(present, inside * penalty, 0.0)
        store(dual_v.at[:, at], dual.at[:, at])
    for copy in used:
        copy.wait()


def params(limit, **more):
    return pltpu.CompilerParams(vmem_limit_bytes=limit * MIB, **more)


def on_device(weight, readings, missing, left_init, right_init):
    rows, times = readings.shape
    shape = jax.ShapeDtypeStruct
    full = shape((rows, times), F32)
    dma = pltpu.SemaphoreType.DMA
    in_vmem = pl.BlockSpec(memory_space=VMEM)
    in_hbm = pl.BlockSpec(memory_space=pltpu.HBM)
    chunked = (2, 4, 4, RANK, LANES)
    seen, clipped, left, right, sums, inverse = pl.pallas_call(
        functools.partial(factorize, weight),
        out_shape=[full, full, shape((2, RANK, rows), F32), shape(chunked, F32), shape((8, LANES), F32),
                   shape((2, RANK, RANK), F32)],
        in_specs=[in_hbm] * 4,
        out_specs=[in_vmem] * 6,
        scratch_shapes=[
            VMEM((rows, times), jnp.int32),
            VMEM((rows, times), BF16),
            VMEM((rows, times), BF16),
            VMEM((rows, times), BF16),
            VMEM((RANK, times), F32),
            VMEM((RANK, rows), F32),
            VMEM((rows, 3 * RANK), F32),
            VMEM((3 * RANK, 3 * RANK), F32),
            VMEM((8, LANES), F32),
            VMEM((2, 32, LANES), F32),
            VMEM((2, 3, 32, LANES), F32),
            VMEM((2, 136, LANES), F32),
            VMEM((2, 3, 136, LANES), F32),
            VMEM((2, 3, 40, LANES), F32),
            VMEM((2, 40, LANES), F32),
            VMEM((2, 3, 40, LANES), F32),
            VMEM((2, 3, 40, LANES), F32),
            VMEM((2,) + chunked, F32),
            VMEM((2, 4, 4, RANK, LANES), F32),
            VMEM((2, 15, RANK, LANES), F32),
            VMEM(chunked, F32),
            VMEM((RANK, times), F32),
            VMEM((2, 32, LANES), F32),
            dma((2, 43 + 60 * PARTS)),
            dma((18,)),
        ],
        compiler_params=params(40, collective_id=0, has_side_effects=True),
    )(*(pltpu.with_memory_space_constraint(arg, pltpu.HBM) for arg in (readings, missing, left_init.T, right_init.T)))
    sparse, dual, right_t, left_t = pl.pallas_call(
        functools.partial(last_pass, weight),
        out_shape=[full, full, shape((RANK, times), F32), shape((RANK, rows), F32)],
        in_specs=[in_vmem] * 6,
        out_specs=[in_hbm] * 4,
        scratch_shapes=[VMEM((rows, times), F32), VMEM((rows, times), F32), VMEM((RANK, times), F32), dma((25,))],
        compiler_params=params(24),
    )(seen, clipped, left, right, sums, inverse)
    return left_t.T, right_t.T, sparse, dual


def solution(mesh):
    weight = 1.0 / math.sqrt(max(8192, 16384))
    in_specs = (P("sys", "tm"), P("sys", "tm"), P("sys", None), P("tm", None))
    out_specs = (P("sys", None), P("tm", None), P("sys", "tm"), P("sys", "tm"))
    return jax.shard_map(
        functools.partial(on_device, weight), mesh=mesh, in_specs=in_specs, out_specs=out_specs, check_vma=False
    )
```
